32 devices in a mesh: section: 2 (over x), row: 4 (over z), col: 4 (over y, core).
Axes of the slice: x: 2, y: 2, z: 4, core: 2. Of those that a mesh axis runs over, the one named last changes fastest.
Arguments:
- boundary: bfloat16 [2, 4, 512, 2048], P('section', None, 'row', 'col'), may hold values from -6 to 6
- segment_ids: int32 [4, 512], replicated, may hold values from -1 to 1, as said below
- w_query: bfloat16 [2, 2048, 2048], P('section', 'row', 'col'), may hold values from -0.125 to 0.125
- key_projection: bfloat16 [2, 2048, 1024], P('section', 'row', 'col'), may hold values from -0.125 to 0.125
- value_projection: bfloat16 [2, 2048, 1024], P('section', 'row', 'col'), may hold values from -0.125 to 0.125
- w_out: bfloat16 [2, 2048, 2048], P('section', 'col', 'row'), may hold values from -0.375 to 0.375
- w_gate: bfloat16 [2, 2048, 6144], P('section', 'row', 'col'), may hold values from -0.125 to 0.125
- w_up: bfloat16 [2, 2048, 6144], P('section', 'row', 'col'), may hold values from -0.125 to 0.125
- w_down: bfloat16 [2, 6144, 2048], P('section', 'col', 'row'), may hold values from -0.078125 to 0.078125
- attn_gain: bfloat16 [2, 2048], P('section', 'col'), may hold values from 0.5 to 1.5
- mlp_gain: bfloat16 [2, 2048], P('section', 'col'), may hold values from 0.5 to 1.5
- query_gain: bfloat16 [2, 128], P('section'), may hold values from 0.5 to 1.5
- key_norm_gain: bfloat16 [2, 128], P('section'), may hold values from 0.5 to 1.5
Outputs:
- section_out: float32 [2, 4, 512, 2048], P('section', None, 'row', 'col')
- grad_query: float32 [2, 2048, 2048], P('section', 'row', 'col')
- grad_key: float32 [2, 2048, 1024], P('section', 'row', 'col')
- grad_value: float32 [2, 2048, 1024], P('section', 'row', 'col')
- grad_out: float32 [2, 2048, 2048], P('section', 'col', 'row')
- grad_gate: float32 [2, 2048, 6144], P('section', 'row', 'col')
- grad_up: float32 [2, 2048, 6144], P('section', 'row', 'col')
- grad_down: float32 [2, 6144, 2048], P('section', 'col', 'row')
- grad_attn_gain: float32 [2, 2048], P('section')
- grad_mlp_gain: float32 [2, 2048], P('section')
- grad_query_gain: float32 [2, 128], P('section')
- grad_key_gain: float32 [2, 128], P('section')
The draws below stay inside these ranges and needn't reach their ends.
Inputs may be any that keep to these rules, and one draw needn't show every extreme that they name: `segment_ids`: in each micro-batch the ids are 0 on a first run of slots, then possibly 1 on a second run, then -1 on an empty tail; at least 256 slots of each micro-batch hold tokens, and in at least one micro-batch a single sequence fills all 512 slots.
All inputs are finite; a program needn't handle non-finite values.
Results may differ from the reference program's by a relative error of at most 0.025.
Values may be sent and summed in bfloat16 or wider, within the bound.
No kernel may reach another device: no remote copies, remote signals or barrier semaphores. Data moves between devices by JAX's collectives and lax.ppermute only.
A program may use at most 192 MiB of HBM per device.

```python
import jax
import jax.numpy as jnp
from jax import lax

MODEL_DIMENSION = 2048
QUERY_HEADS = 16
KEY_VALUE_HEADS = 8
HEAD_SIZE = 128
FF = 6144
MB = 4
CAP = 512


def draw_segment_ids(key, part):
    key = jax.random.fold_in(key, 11)
    key_fill, key_split, key_full = jax.random.split(key, 3)
    half_cap = CAP // 2
    fill_len = jax.random.randint(key_fill, (MB,), half_cap, CAP + 1)
    split_at = jax.random.randint(key_split, (MB,), half_cap, CAP + 1)
    chosen = jnp.arange(MB) == jax.random.randint(key_full, (), 0, MB)
    fill_len = jnp.where(chosen, CAP, fill_len)
    split_at = jnp.where(chosen, CAP, split_at)
    places = jnp.arange(CAP)[None, :]
    segments = jnp.where(places < split_at[:, None], 0, 1)
    segments = jnp.where(places < fill_len[:, None], segments, -1)
    return segments.astype(jnp.int32)


def level_of(rng, shape, cuts, smallest, high):
    def one(position, blocks):
        draws = jax.random.uniform(jax.random.fold_in(jax.random.fold_in(rng, 6), position), (blocks,), jnp.float32, smallest / len(cuts), high / len(cuts))
        return jnp.repeat(jnp.exp(draws), shape[position] // blocks).reshape((-1,) + (1,) * (len(shape) - position - 1))

    factor_of = one(*cuts[0])
    for cut in cuts[1:]:
        factor_of = factor_of * one(*cut)
    return factor_of


def gaussian(own_key, shape, deviation, most, shards=(), kind=jnp.bfloat16):
    loudness = level_of(own_key, shape, shards, -0.22, 0.18) if shards else 1.0
    result = jax.random.normal(own_key, shape, jnp.float32) * deviation * loudness
    return jnp.minimum(jnp.maximum(result, -most), most).astype(kind)


def setup_inputs(seed: int = 0) -> dict:
    keys = jax.random.split(jax.random.key(seed), 14)
    return {
        "boundary": gaussian(keys[0], (2, MB, CAP, MODEL_DIMENSION), 1.0, 6.0, ((0, 2), (2, 4), (3, 4))),
        "segment_ids": draw_segment_ids(jax.random.fold_in(keys[13], 71), 0),
        "w_query": gaussian(keys[2], (2, MODEL_DIMENSION, QUERY_HEADS * HEAD_SIZE), MODEL_DIMENSION ** -0.5, 0.125, ((0, 2), (1, 4), (2, 4))),
        "key_projection": gaussian(keys[3], (2, MODEL_DIMENSION, KEY_VALUE_HEADS * HEAD_SIZE), MODEL_DIMENSION ** -0.5, 0.125, ((0, 2), (1, 4), (2, 4))),
        "value_projection": gaussian(keys[4], (2, MODEL_DIMENSION, KEY_VALUE_HEADS * HEAD_SIZE), MODEL_DIMENSION ** -0.5, 0.125, ((0, 2), (1, 4), (2, 4))),
        "w_out": gaussian(keys[5], (2, QUERY_HEADS * HEAD_SIZE, MODEL_DIMENSION), (QUERY_HEADS * HEAD_SIZE // 8) ** -0.5, 0.375, ((0, 2), (1, 4), (2, 4))),
        "w_gate": gaussian(keys[6], (2, MODEL_DIMENSION, FF), MODEL_DIMENSION ** -0.5, 0.125, ((0, 2), (1, 4), (2, 4))),
        "w_up": gaussian(keys[7], (2, MODEL_DIMENSION, FF), MODEL_DIMENSION ** -0.5, 0.125, ((0, 2), (1, 4), (2, 4))),
        "w_down": gaussian(keys[8], (2, FF, MODEL_DIMENSION), FF ** -0.5, 0.078125, ((0, 2), (1, 4), (2, 4))),
        "attn_gain": jnp.clip(1.0 + 0.1 * jax.random.normal(keys[9], (2, MODEL_DIMENSION), jnp.float32), 0.5, 1.5).astype(jnp.bfloat16),
        "mlp_gain": jnp.clip(1.0 + 0.1 * jax.random.normal(keys[10], (2, MODEL_DIMENSION), jnp.float32), 0.5, 1.5).astype(jnp.bfloat16),
        "query_gain": jnp.clip(1.0 + 0.1 * jax.random.normal(keys[11], (2, HEAD_SIZE), jnp.float32), 0.5, 1.5).astype(jnp.bfloat16),
        "key_norm_gain": jnp.clip(1.0 + 0.1 * jax.random.normal(keys[12], (2, HEAD_SIZE), jnp.float32), 0.5, 1.5).astype(jnp.bfloat16),
    }


EPS = 1e-06
THETA = 1000000.0
TOP_PRECISION = lax.Precision.HIGHEST

@jax.custom_vjp
def lowered_value(v):
    return lax.optimization_barrier(v.astype(jnp.bfloat16)).astype(jnp.float32)

@jax.custom_vjp
def low_back(v):
    return v

def low_keep(v):
    return (lowered_value(v), None)

def low_pass(kept, grad):
    return (grad,)

def back_keep(v):
    return (v, None)

def back_low(kept, grad):
    return (lowered_value(grad),)
lowered_value.defvjp(low_keep, low_pass)
low_back.defvjp(back_keep, back_low)

def positions(segments):
    places = jnp.arange(segments.shape[0], dtype=jnp.int32)
    changed = jnp.concatenate([jnp.ones((1,), bool), segments[1:] != segments[:-1]])
    starts = lax.cummax(jnp.where(changed, places, jnp.zeros_like(places)), axis=0)
    return places - starts

def rotary_tables(offsets, head_width):
    inv_freq = THETA ** (-jnp.arange(0, head_width, 2, dtype=jnp.float32) / head_width)
    angles = offsets.astype(jnp.float32)[:, None] * inv_freq[None, :]
    cosine_table = jnp.concatenate([jnp.cos(angles), jnp.cos(angles)], axis=1)
    sine_lookup = jnp.concatenate([jnp.sin(angles), jnp.sin(angles)], axis=1)
    return (cosine_table, sine_lookup)

def rotate_head_halves(raw_vals, gain_vec, cosine_table, sine_lookup):
    scaled = raw_vals * lax.rsqrt(lax.optimization_barrier(jnp.mean(raw_vals * raw_vals, axis=2, keepdims=True)) + EPS) * gain_vec
    half_width = raw_vals.shape[2] // 2
    turned = jnp.concatenate([-scaled[:, :, half_width:], scaled[:, :, :half_width]], axis=2)
    return scaled * cosine_table[:, None, :] + turned * sine_lookup[:, None, :]

def rms_normed(residual, gain_vec):
    return residual * lax.rsqrt(lax.optimization_barrier(jnp.mean(residual * residual, axis=1, keepdims=True)) + EPS) * gain_vec

def layer_apply(residual, allowed, cosine_table, sine_lookup, params, depth):
    w_query, key_projection, value_projection, w_out, w_gate, w_up, w_down, attn_gain, mlp_gain, query_gain, key_norm_gain = [param[depth] for param in params]
    sequence_length = residual.shape[0]
    normed = lowered_value(rms_normed(residual, attn_gain))
    q_raw = low_back(jnp.dot(normed, w_query, precision=TOP_PRECISION))
    key_unrotated = low_back(jnp.dot(normed, key_projection, precision=TOP_PRECISION))
    value_vectors = lowered_value(low_back(jnp.dot(normed, value_projection, precision=TOP_PRECISION)))
    query_rows = lowered_value(rotate_head_halves(q_raw.reshape(sequence_length, QUERY_HEADS, HEAD_SIZE), query_gain, cosine_table, sine_lookup))
    query_rows = query_rows.reshape(sequence_length, KEY_VALUE_HEADS, QUERY_HEADS // KEY_VALUE_HEADS, HEAD_SIZE)
    key_matrix_rows = lowered_value(rotate_head_halves(key_unrotated.reshape(sequence_length, KEY_VALUE_HEADS, HEAD_SIZE), key_norm_gain, cosine_table, sine_lookup))
    scores = low_back(jnp.einsum('qhgd,khd->hgqk', query_rows, key_matrix_rows, precision=TOP_PRECISION) * HEAD_SIZE ** (-0.5))
    scores = jnp.where(allowed[None, None], scores, -1e+30)
    row_peak = lax.optimization_barrier(jnp.max(scores, axis=3, keepdims=True))
    exp_vals = jnp.exp(scores - row_peak)
    attention_mixing = lowered_value(exp_vals / lax.optimization_barrier(jnp.sum(exp_vals, axis=3, keepdims=True)))
    heads_mixed_output = jnp.einsum('fmvc,cfn->vfmn', attention_mixing, value_vectors.reshape(sequence_length, KEY_VALUE_HEADS, HEAD_SIZE), precision=TOP_PRECISION)
    heads_mixed_output = lowered_value(low_back(heads_mixed_output)).reshape(sequence_length, QUERY_HEADS * HEAD_SIZE)
    middle = residual + low_back(jnp.dot(heads_mixed_output, w_out, precision=TOP_PRECISION))
    normed_m = lowered_value(rms_normed(middle, mlp_gain))
    gate_pre = low_back(jnp.dot(normed_m, w_gate, precision=TOP_PRECISION))
    up_proj = low_back(jnp.dot(normed_m, w_up, precision=TOP_PRECISION))
    hidden = lowered_value(jax.nn.silu(gate_pre) * up_proj)
    return middle + low_back(jnp.dot(hidden, w_down, precision=TOP_PRECISION))

def two_layers(inputs, segments, params):
    places = jnp.arange(segments.shape[0], dtype=jnp.int32)
    allowed = (segments[:, None] == segments[None, :]) & (places[None, :] <= places[:, None])
    cosine_table, sine_lookup = rotary_tables(positions(segments), HEAD_SIZE)
    between = layer_apply(inputs, allowed, cosine_table, sine_lookup, params, 0)
    between = lowered_value(low_back(between))
    return layer_apply(between, allowed, cosine_table, sine_lookup, params, 1)

def reference(boundary, segment_ids, w_query, key_projection, value_projection, w_out, w_gate, w_up, w_down, attn_gain, mlp_gain, query_gain, key_norm_gain):
    inputs = boundary[0].astype(jnp.float32)
    valid = (segment_ids >= 0).astype(jnp.float32)
    upstream = boundary[1].astype(jnp.float32) * valid[:, :, None]
    params = tuple((param.astype(jnp.float32) for param in (w_query, key_projection, value_projection, w_out, w_gate, w_up, w_down, attn_gain, mlp_gain, query_gain, key_norm_gain)))

    def whole_run(inputs, params):

        def one_batch(pair_in):
            return jax.checkpoint(two_layers)(pair_in[0], pair_in[1], params)
        return lax.map(one_batch, (inputs, segment_ids))
    output, pull_back = jax.vjp(whole_run, inputs, params)
    grad_inputs, grads = pull_back(upstream)
    return (jnp.stack([grad_inputs, output]), grads[0], grads[1], grads[2], grads[3], grads[4], grads[5], grads[6], grads[7], grads[8], grads[9], grads[10])
```

```python
import jax
import jax.numpy as jnp
import numpy as np
from jax import lax
from jax.sharding import Mesh
from jax.sharding import PartitionSpec as P

EPS = 1e-06
THETA = 1000000.0
f32 = jnp.float32
bf16 = jnp.bfloat16


def swap(value, axis):
    return lax.ppermute(value, axis, [(0, 1), (1, 0)])


def take(value, index, axis=0):
    return lax.dynamic_index_in_dim(value, index, axis, keepdims=False)


def pair(bit, mine, other, axis=0):
    low = jnp.where(bit == 0, mine, other)
    high = jnp.where(bit == 0, other, mine)
    return jnp.stack([low, high], axis)


def dot(left, right):
    return jnp.dot(left, right, preferred_element_type=f32)


def dot_t(left, right):
    return lax.dot_general(left, right, (((1,), (1,)), ((), ())), preferred_element_type=f32)


def t_dot(left, right):
    return lax.dot_general(left, right, (((0,), (0,)), ((), ())), preferred_element_type=f32)


def gather_tokens(mine):
    part = mine.shape[0] // 2
    low, high = mine[:part], mine[part:]
    near = jnp.concatenate([swap(low, "s"), swap(high, "t")])
    mine_k = swap(mine, "k")
    far_low = swap(jnp.concatenate([low, near[:part]]), "t")
    far_high = swap(jnp.concatenate([high, near[part:]]), "s")
    near_k = swap(near, "k")
    far = jnp.concatenate([far_low, far_high])
    far_k = swap(far, "k")
    return jnp.concatenate([mine, near, far, mine_k, near_k, far_k])


def slots_of(s, t, k, g, groups, part):
    pieces = []
    tok = 4 * part
    for dk in (0, 1):
        for ds, dt, p in (
            (0, 0, 0), (0, 0, 1), (1, 0, 0), (0, 1, 1),
            (0, 1, 0), (1, 1, 0), (1, 0, 1), (1, 1, 1),
        ):
            block = ((s ^ ds) * 2 + (t ^ dt)) * groups + g
            start = block * tok + (k ^ dk) * (2 * part) + p * part
            pieces.append(start + jnp.arange(part, dtype=jnp.int32))
    return jnp.concatenate(pieces)


def scatter_sum(near_part, far_part):
    total = near_part + swap(far_part, "k").astype(f32)
    part = total.shape[0] // 8
    far = total[4 * part :].astype(bf16)
    from_t = swap(far[: 2 * part], "t").astype(f32)
    from_s = swap(far[2 * part :], "s").astype(f32)
    x0 = (total[2 * part : 3 * part] + from_t[part:]).astype(bf16)
    y1 = (total[3 * part : 4 * part] + from_s[part:]).astype(bf16)
    back_s = swap(x0, "s").astype(f32)
    back_t = swap(y1, "t").astype(f32)
    low = total[:part] + from_t[:part] + back_s
    high = total[part : 2 * part] + from_s[:part] + back_t
    return jnp.concatenate([low, high])


def split_product(left, right, contract):
    half = left.shape[0] // 2
    far = contract(left[half:], right).astype(bf16)
    near = contract(left[:half], right)
    return near, far


def rms(residual):
    return lax.rsqrt(jnp.mean(residual * residual, axis=1, keepdims=True) + EPS)


def norm_back(residual, scale, gain, grad):
    lifted = grad * gain
    inner = jnp.mean(lifted * residual, axis=1, keepdims=True)
    grad_residual = scale * lifted - residual * (scale**3 * inner)
    return grad_residual, jnp.sum(grad * residual * scale, axis=0)


def rotate(raw, gain, cosine, sine):
    scaled = raw * lax.rsqrt(jnp.mean(raw * raw, axis=2, keepdims=True) + EPS) * gain
    half = raw.shape[2] // 2
    turned = jnp.concatenate([-scaled[:, :, half:], scaled[:, :, :half]], axis=2)
    return scaled * cosine[:, None, :] + turned * sine[:, None, :]


def body(
    boundary, segment_ids, w_query, key_projection, value_projection, w_out, w_gate, w_up, w_down,
    attn_gain, mlp_gain, query_gain, key_norm_gain,
):
    s, h, t, g, y, k = (lax.axis_index(name) for name in ("s", "h", "t", "g", "y", "k"))
    groups = lax.axis_size("g")
    micro, tok, width = boundary.shape[1:]
    cols = lax.axis_size("y") * lax.axis_size("k")
    model = width * cols
    head = query_gain.shape[1]
    span = segment_ids.shape[1]
    rb = w_query.shape[1]
    q_part = w_query.shape[2] // 4
    ff_part = w_gate.shape[2] // 4
    scale_qk = head ** (-0.5)

    packed = jnp.concatenate([attn_gain[0], mlp_gain[0], query_gain[0], key_norm_gain[0]])
    packed = lax.all_gather(packed, ("s", "y", "k"), axis=0).reshape(2, cols, -1).astype(f32)
    gain_a = packed[:, :, :width].reshape(2, model)
    gain_m = packed[:, :, width : 2 * width].reshape(2, model)
    gain_q = packed[:, 0, 2 * width : 2 * width + head]
    gain_k = packed[:, 0, 2 * width + head :]

    sent = boundary[0].reshape(2, 2, 2, tok // 2, width).transpose(0, 2, 1, 3, 4)
    sent = lax.all_to_all(sent.reshape(cols, 2, tok // 2, width), ("y", "k"), 0, 0, tiled=True)
    rows = sent.transpose(1, 2, 0, 3).reshape(2, tok // 2, model)
    own_rows = take(rows, h)
    other_rows = swap(take(rows, 1 - h), "h")
    keep = jnp.where(s == h, own_rows, other_rows)
    passed = swap(jnp.where(s == h, other_rows, own_rows), "s")
    entering = jnp.where(s == 0, keep, passed).astype(f32)
    cotangent = jnp.where(s == 0, passed, keep).astype(f32)

    def across(own):
        other = swap(take(own, 1 - s), "s")
        own = take(own, s)
        return [jnp.where(s == layer, own, other) for layer in (0, 1)]

    def spread(value):
        mine = pair(t, take(value, t), swap(take(value, 1 - t), "t"))
        mine = pair(h, mine, swap(mine, "h"))
        if groups > 1:
            mine = lax.all_gather(mine, "g", axis=2)
        mine = mine.reshape((-1,) + value.shape[1:])
        return mine, swap(mine, "y")

    def spread_kv(value):
        mine = pair(h, value, swap(value, "h"))
        if groups > 1:
            mine = lax.all_gather(mine, "g", axis=1)
        mine = jnp.stack([mine, swap(mine, "y")])
        return pair(t, mine, swap(mine, "t"), 2)

    def by_columns(weight):
        return weight.reshape(rb, 2, 2, -1).transpose(1, 2, 0, 3)

    def by_rows(weight):
        return weight.reshape(2, 2, -1, rb)

    kv_home = jnp.stack(
        [key_projection[0].reshape(rb, 2, head), value_projection[0].reshape(rb, 2, head)], 2
    )
    kv_home = kv_home.transpose(1, 0, 2, 3).reshape(2, rb, 2 * head)
    q_home = by_columns(w_query[0])
    o_home = by_rows(w_out[0])
    gu_home = jnp.concatenate([by_columns(w_gate[0]), by_columns(w_up[0])], 3)
    d_home = by_rows(w_down[0])

    q_half = across(q_home)
    kv_half = across(kv_home)
    o_half = across(o_home)
    gu_half = across(gu_home)
    d_half = across(d_home)

    def columns(pieces):
        return jnp.concatenate([piece.reshape(model, -1) for piece in pieces], 1)

    def rows_of(pieces):
        return jnp.concatenate(
            [piece.transpose(1, 0, 2).reshape(piece.shape[1], model) for piece in pieces], 0
        )

    def layer_weights(layer):
        wq = spread(q_half[layer])
        wkv = spread_kv(kv_half[layer])
        if groups > 1:
            wkv = wkv.transpose(0, 1, 2, 3, 4, 5)
        wkv = wkv.reshape(2, model, 2 * head)
        w_in = jnp.concatenate(
            [
                wq[0].reshape(model, -1), wq[1].reshape(model, -1),
                wkv[0, :, :head], wkv[1, :, :head], wkv[0, :, head:], wkv[1, :, head:],
            ],
            1,
        )
        wo = rows_of(spread(o_half[layer]))
        wgu = columns(spread(gu_half[layer]))
        wd = rows_of(spread(d_half[layer]))
        return w_in, wo, wgu, wd

    weights = [layer_weights(layer) for layer in (0, 1)]

    segments = take(segment_ids, 2 * y + h)
    part = tok // 4
    slots = slots_of(s, t, k, g, groups, part)
    places = jnp.arange(span, dtype=jnp.int32)
    changed = jnp.concatenate([jnp.ones((1,), bool), segments[1:] != segments[:-1]])
    starts = lax.cummax(jnp.where(changed, places, 0), axis=0)
    offsets = (places - starts)[slots]
    my_segments = segments[slots]
    inv_freq = THETA ** (-jnp.arange(0, head, 2, dtype=f32) / head)
    angles = offsets.astype(f32)[:, None] * inv_freq[None, :]
    cosine = jnp.concatenate([jnp.cos(angles)] * 2, 1)
    sine = jnp.concatenate([jnp.sin(angles)] * 2, 1)
    valid = (my_segments[: 2 * part] >= 0).astype(f32)
    if groups > 1:
        key_slots = lax.all_gather(slots, "g", axis=0, tiled=True)
        key_segments = segments[key_slots]
    else:
        key_slots, key_segments = slots, my_segments
    allowed = (my_segments[:, None] == key_segments[None, :]) & (
        key_slots[None, :] <= slots[:, None]
    )
    q_cols = 2 * head

    def all_keys(value):
        return lax.all_gather(value, "g", axis=0, tiled=True) if groups > 1 else value

    def sum_keys(value):
        if groups > 1:
            return lax.psum_scatter(value.astype(bf16), "g", scatter_dimension=0, tiled=True).astype(f32)
        return value

    def scores_of(q, keys):
        scores = jnp.einsum("qhd,khd->hqk", q, keys, preferred_element_type=f32) * scale_qk
        return jnp.where(allowed[None], scores, -1e30)

    def heads_of(value):
        return value.reshape(value.shape[0], 2, head)

    def forward(layer, residual):
        w_in, wo, wgu, wd = weights[layer]
        scale_a = rms(residual)
        xa = gather_tokens((residual * scale_a * gain_a[layer]).astype(bf16))
        raw = dot(xa, w_in)
        q_raw, k_raw = heads_of(raw[:, :q_cols]), heads_of(raw[:, q_cols : 2 * q_cols])
        v = heads_of(raw[:, 2 * q_cols :]).astype(bf16)
        q = rotate(q_raw, gain_q[layer], cosine, sine).astype(bf16)
        keys = rotate(k_raw, gain_k[layer], cosine, sine).astype(bf16)
        keys, values = all_keys(keys), all_keys(v)
        scores = scores_of(q, keys)
        peak = jnp.max(scores, axis=2, keepdims=True)
        exps = jnp.exp(scores - peak)
        denom = jnp.sum(exps, axis=2, keepdims=True)
        mixing = (exps / denom).astype(bf16)
        lse = peak + jnp.log(denom)
        o = jnp.einsum("hqk,khd->qhd", mixing, values, preferred_element_type=f32)
        o = o.astype(bf16).reshape(-1, q_cols)
        middle = residual + scatter_sum(*split_product(o, wo, dot))
        scale_m = rms(middle)
        xm = gather_tokens((middle * scale_m * gain_m[layer]).astype(bf16))
        gu = dot(xm, wgu).reshape(xm.shape[0], 2, 2, ff_part)
        gate, up = gu[:, :, 0], gu[:, :, 1]
        act = (gate * jax.nn.sigmoid(gate) * up).astype(bf16).reshape(-1, 2 * ff_part)
        result = middle + scatter_sum(*split_product(act, wd, dot))
        kept = (residual, scale_a, xa, q_raw, k_raw, q, keys, values, lse, o, middle, scale_m, xm, gate, up, act)
        return result, kept

    def reduce_blocks(own, other, axis):
        def blocks(value):
            shape = value.shape[:axis] + (2, 2, groups, rb) + value.shape[axis + 1 :]
            return jnp.moveaxis(value.reshape(shape), (axis, axis + 1, axis + 2), (0, 1, 2))

        total = blocks(own + swap(other.astype(bf16), "y").astype(f32))
        if groups > 1:
            total = lax.psum_scatter(total.astype(bf16), "g", scatter_dimension=2, tiled=True).astype(f32)
        total = total[:, :, 0]
        return take(total, h) + swap(take(total, 1 - h).astype(bf16), "h").astype(f32)

    def back(own, other, axis):
        total = reduce_blocks(own, other, axis).astype(bf16)
        return pair(t, take(total, t), swap(take(total, 1 - t), "t"))

    def back_kv(own, other):
        def blocks(value):
            return value.reshape(2, 2, groups, rb, -1)

        total = jnp.stack([blocks(own), blocks(other)])
        total = take(total, t, 2) + swap(take(total, 1 - t, 2).astype(bf16), "t").astype(f32)
        total = total[0] + swap(total[1].astype(bf16), "y").astype(f32)
        if groups > 1:
            total = lax.psum_scatter(total.astype(bf16), "g", scatter_dimension=1, tiled=True).astype(f32)
        total = total[:, 0]
        total = take(total, h) + swap(take(total, 1 - h).astype(bf16), "h").astype(f32)
        return total.astype(bf16)

    def backward(layer, grad_top, kept):
        w_in, wo, wgu, wd = weights[layer]
        (residual, scale_a, xa, q_raw, k_raw, q, keys, values, lse, o, middle, scale_m, xm, gate, up, act) = kept
        g3 = gather_tokens(grad_top.astype(bf16))
        d_down = t_dot(act, g3)
        d_act = dot_t(g3, wd).reshape(-1, 2, ff_part)
        sig = jax.nn.sigmoid(gate)
        d_gate = (d_act * up * sig * (1 + gate * (1 - sig))).astype(bf16)
        d_up = (d_act * gate * sig).astype(bf16)
        d_gu = jnp.stack([d_gate, d_up], 2).reshape(-1, 4 * ff_part)
        d_xm = scatter_sum(*split_product(d_gu, wgu, dot_t))
        grad_gu = t_dot(xm, d_gu)
        half = 2 * ff_part
        home_down = back(d_down[:ff_part], d_down[ff_part:], 1)
        home_gu = back(grad_gu[:, :half], grad_gu[:, half:], 0)
        d_mid, d_gain_m = norm_back(middle, scale_m, gain_m[layer], d_xm)
        d_mid = grad_top + d_mid
        g2 = gather_tokens(d_mid.astype(bf16))
        d_out = t_dot(o, g2)
        home_out = back(d_out[:q_part], d_out[q_part:], 1)
        d_o = heads_of(dot_t(g2, wo).astype(bf16))
        mixing = jnp.exp(scores_of(q, keys) - lse)
        d_mix = jnp.einsum("qhd,khd->hqk", d_o, values, preferred_element_type=f32)
        inner = jnp.sum(mixing * d_mix, axis=2, keepdims=True)
        d_scores = (mixing * (d_mix - inner)).astype(bf16)
        d_q = jnp.einsum("hqk,khd->qhd", d_scores, keys, preferred_element_type=f32) * scale_qk
        d_k = jnp.einsum("hqk,qhd->khd", d_scores, q, preferred_element_type=f32) * scale_qk
        d_v = jnp.einsum("hqk,qhd->khd", mixing.astype(bf16), d_o, preferred_element_type=f32)
        d_k, d_v = sum_keys(d_k), sum_keys(d_v)
        _, pull_q = jax.vjp(lambda raw, gain: rotate(raw, gain, cosine, sine), q_raw, gain_q[layer])
        _, pull_k = jax.vjp(lambda raw, gain: rotate(raw, gain, cosine, sine), k_raw, gain_k[layer])
        d_q_raw, d_gain_q = pull_q(d_q)
        d_k_raw, d_gain_k = pull_k(d_k)
        d_raw = jnp.concatenate(
            [value.astype(bf16).reshape(-1, q_cols) for value in (d_q_raw, d_k_raw, d_v)], 1
        )
        d_xa = scatter_sum(*split_product(d_raw, w_in, dot_t))
        grad_in = t_dot(xa, d_raw)
        home_q = back(grad_in[:, :head], grad_in[:, head:q_cols], 0)
        grad_k0, grad_k1 = grad_in[:, 2 * head : 3 * head], grad_in[:, 3 * head : 4 * head]
        grad_v0, grad_v1 = grad_in[:, 4 * head : 5 * head], grad_in[:, 5 * head :]
        home_kv = back_kv(
            jnp.concatenate([grad_k0, grad_v0], 1), jnp.concatenate([grad_k1, grad_v1], 1)
        )
        d_res, d_gain_a = norm_back(residual, scale_a, gain_a[layer], d_xa)
        homes = (home_q, home_kv, home_out, home_gu, home_down)
        return d_mid + d_res, homes, (d_gain_a, d_gain_m, d_gain_q, d_gain_k)

    middle, kept0 = forward(0, entering)
    output, kept1 = forward(1, middle.astype(bf16).astype(f32))
    grad, homes1, gains1 = backward(1, cotangent * valid[:, None], kept1)
    grad, homes0, gains0 = backward(0, grad.astype(bf16).astype(f32), kept0)

    def home(index):
        low, high = homes0[index], homes1[index]
        mine = jnp.where(s == 0, low, high)
        other = swap(jnp.where(s == 0, high, low), "s")
        return pair(s, mine, other)

    full_q = home(0).transpose(2, 0, 1, 3).reshape(rb, -1)
    full_kv = home(1).reshape(2, rb, 2, head).transpose(2, 1, 0, 3).reshape(2, rb, -1)
    full_out = home(2).reshape(-1, rb)
    full_gu = home(3).reshape(2, 2, rb, 2, ff_part).transpose(3, 2, 0, 1, 4).reshape(2, rb, -1)
    full_down = home(4).reshape(-1, rb)

    low, high = grad.astype(bf16), output.astype(bf16)
    keep = jnp.where(s == 0, low, high)
    passed = swap(jnp.where(s == 0, high, low), "s")
    mine = jnp.where(s == h, keep, passed)
    other = swap(jnp.where(s == h, passed, keep), "h")
    rows = pair(h, mine, other).reshape(2, tok // 2, cols, width).transpose(2, 0, 1, 3)
    rows = lax.all_to_all(rows, ("y", "k"), 0, 0, tiled=True)
    rows = rows.reshape(2, 2, 2, tok // 2, width).transpose(0, 2, 1, 3, 4)
    section_out = rows.reshape(micro, tok, width)

    sums = jnp.concatenate([value for gains in (gains0, gains1) for value in gains])
    sums = take(lax.psum(sums, ("s", "h", "t", "g", "y", "k")).reshape(2, -1), s)
    return (
        section_out.astype(f32)[None],
        full_q.astype(f32)[None],
        full_kv[0].astype(f32)[None],
        full_kv[1].astype(f32)[None],
        full_out.astype(f32)[None],
        full_gu[0].astype(f32)[None],
        full_gu[1].astype(f32)[None],
        full_down.astype(f32)[None],
        sums[None, :model],
        sums[None, model : 2 * model],
        sums[None, 2 * model : 2 * model + head],
        sums[None, 2 * model + head :],
    )


def solution(mesh):
    sections, row_count, col_count = (mesh.shape[name] for name in ("section", "row", "col"))
    shape = (sections, 2, 2, row_count // 4, 2, col_count // 2)
    mesh = Mesh(np.asarray(mesh.devices).reshape(shape), ("s", "h", "t", "g", "y", "k"))
    row, col = ("h", "t", "g"), ("y", "k")
    in_row, in_col = P("s", row, col), P("s", col, row)
    return jax.shard_map(
        body,
        mesh=mesh,
        in_specs=(
            P("s", None, row, col), P(), in_row, in_row, in_row, in_col, in_row, in_row, in_col,
            P("s", col), P("s", col), P("s", None), P("s", None),
        ),
        out_specs=(
            P("s", None, row, col), in_row, in_row, in_row, in_col, in_row, in_row, in_col,
            P("s", None), P("s", None), P("s", None), P("s", None),
        ),
        check_vma=False,
    )
```

```python
import jax
import jax.numpy as jnp
import numpy as np
from jax import lax
from jax.experimental.layout import Layout, with_layout_constraint
from jax.sharding import Mesh
from jax.sharding import PartitionSpec as P

EPS = 1e-06
THETA = 1000000.0
f32 = jnp.float32
bf16 = jnp.bfloat16


def swap(value, axis):
    return lax.ppermute(value, axis, [(0, 1), (1, 0)])


def exchange(value, axes):
    return lax.all_to_all(value, axes, 0, 0, tiled=True)


def take(value, index, axis=0):
    return lax.dynamic_index_in_dim(value, index, axis, keepdims=False)


def pair(bit, mine, other, axis=0):
    low = jnp.where(bit == 0, mine, other)
    high = jnp.where(bit == 0, other, mine)
    return jnp.stack([low, high], axis)


def plain(value):
    return with_layout_constraint(value, Layout(major_to_minor=tuple(range(value.ndim))))


def dot(left, right):
    return jnp.dot(left, right, preferred_element_type=f32)


def dot_t(left, right):
    return lax.dot_general(left, right, (((1,), (1,)), ((), ())), preferred_element_type=f32)


def t_dot(left, right):
    return lax.dot_general(left, right, (((0,), (0,)), ((), ())), preferred_element_type=f32)


def cross(value):
    return lax.ppermute(value, ("s", "t"), [(i, 3 - i) for i in range(4)])


def gather_tokens(mine, middle):
    core = jnp.concatenate([mine, swap(mine, "s"), swap(mine, "t"), cross(mine)])
    core = middle(core)
    return jnp.concatenate([core, swap(core, "k")])


def slots_of(s, t, k, g, groups, part):
    pieces = []
    for dk in (0, 1):
        for ds, dt in ((0, 0), (1, 0), (0, 1), (1, 1)):
            block = ((s ^ ds) * 2 + (t ^ dt)) * groups + g
            start = block * (2 * part) + (k ^ dk) * part
            pieces.append(start + jnp.arange(part, dtype=jnp.int32))
    return jnp.concatenate(pieces)


def scatter_sum(near, far, middle):
    total = near + swap(far, "k").astype(f32)
    part = total.shape[0] // 4
    total, far = middle((total[:part], total[part:].astype(bf16)))
    pieces = [swap(far[:part], "s"), swap(far[part : 2 * part], "t"), cross(far[2 * part :])]
    return total + sum(piece.astype(f32) for piece in pieces)


def split_product(lefts, rights):
    half = lefts[0].shape[0] // 2
    far = sum(dot_t(left[half:], right) for left, right in zip(lefts, rights)).astype(bf16)
    near = sum(dot_t(left[:half], right) for left, right in zip(lefts, rights))
    return near, far


class Clock:
    def __init__(self):
        self.plans, self.flying, self.ready = {}, {}, {}

    def add(self, name, begin, end, make, send):
        self.plans[name] = (begin, end, make, send)

    def point(self, label, chain):
        ends = [name for name, plan in self.plans.items() if plan[1] == label]
        if ends:
            chain, arrived = lax.optimization_barrier((chain, [self.flying[name] for name in ends]))
            self.ready.update(zip(ends, arrived))
        begins = [name for name, plan in self.plans.items() if plan[0] == label]
        if begins:
            values = [self.plans[name][2]() for name in begins]
            chain, values = lax.optimization_barrier((chain, values))
            for name, value in zip(begins, values):
                self.flying[name] = self.plans[name][3](value)
        return chain


def rms(residual):
    return lax.rsqrt(jnp.mean(residual * residual, axis=1, keepdims=True) + EPS)


def norm_back(residual, scale, gain, grad):
    lifted = grad * gain
    inner = jnp.mean(lifted * residual, axis=1, keepdims=True)
    grad_residual = scale * lifted - residual * (scale**3 * inner)
    return grad_residual, jnp.sum(grad * residual * scale, axis=0)


def rotate(raw, gain, cosine, sine):
    scaled = raw * lax.rsqrt(jnp.mean(raw * raw, axis=2, keepdims=True) + EPS) * gain
    half = raw.shape[2] // 2
    turned = jnp.concatenate([-scaled[:, :, half:], scaled[:, :, :half]], axis=2)
    return scaled * cosine[:, None, :] + turned * sine[:, None, :]


FETCH = {
    "a": ("in", "rows"),
    "m0": ("c1", "c2"),
    "m1": ("c2", "F03"),
}
SPREAD = {
    "a00": ("rows", "c1", "c1", "c2"),
    "a10": ("c1", "c2", "c2", "c3"),
    "m00": ("c2", "c3", "c3", "F03"),
    "m20": ("c3", "F03", "F03", "F05"),
    "m10": ("F03", "F05", "F05", "F06"),
    "m30": ("F05", "F06", "F06", "F07"),
    "a01": ("F06", "F07", "F07", "F10"),
    "a11": ("F07", "F10", "F10", "F11"),
    "m01": ("F10", "F11", "F11", "F13"),
    "m21": ("F11", "F13", "F13", "F15"),
    "m11": ("F13", "F15", "F15", "F16"),
    "m31": ("F15", "F16", "F16", "F17"),
}
RETURN = {
    "m01": ("B14", "B15", "B15", "B16"),
    "m21": ("B15", "B16", "B16", "B18"),
    "m11": ("B16", "B18", "B18", "B00"),
    "m31": ("B18", "B00", "B00", "B01"),
    "a01": ("B00", "B01", "B01", "B03"),
    "a11": ("B01", "B03", "B04", "B05"),
    "m00": ("B04", "B05", "B05", "B06"),
    "m20": ("B05", "B06", "B06", "B08"),
    "m10": ("B06", "B08", "B08", "E0"),
    "m30": ("B08", "E0", "E0", "E1"),
    "a00": ("E0", "E1", "E1", "E2"),
    "a10": ("E1", "E2", "E2", "E3"),
}
HOME = {
    "m0": ("E0", "E1"),
    "m1": ("E1", "E3"),
}


def body(
    boundary, segment_ids, w_query, key_projection, value_projection, w_out, w_gate, w_up, w_down,
    attn_gain, mlp_gain, query_gain, key_norm_gain,
):
    s, h, t, g, y, k = (lax.axis_index(name) for name in ("s", "h", "t", "g", "y", "k"))
    groups = lax.axis_size("g")
    micro, tok, width = boundary.shape[1:]
    cols = lax.axis_size("y") * lax.axis_size("k")
    model = width * cols
    head = query_gain.shape[1]
    span = segment_ids.shape[1]
    rb = w_query.shape[1]
    ff = w_gate.shape[2] // 4
    scale_qk = head ** (-0.5)
    clock = Clock()

    packed = jnp.concatenate([attn_gain[0], mlp_gain[0], query_gain[0], key_norm_gain[0]])[None]

    sent = boundary[0].reshape(2, 2, 2, tok // 2, width).transpose(0, 2, 1, 3, 4)
    sent = exchange(sent.reshape(cols, 2, tok // 2, width), ("y", "k"))
    rows = sent.transpose(1, 2, 0, 3).reshape(2, tok // 2, model)

    def quarters(weight):
        size = weight.shape[1] // 4
        return [weight[:, i * size : (i + 1) * size] for i in range(4)]

    def to_groups(value):
        return exchange(value, ("s", "t"))

    a_home = []
    for i, (q, o) in enumerate(zip(quarters(w_query[0]), quarters(w_out[0].T))):
        low = (i // 2) * head
        kv = [w[0, :, low : low + head] for w in (key_projection, value_projection)]
        a_home.append(jnp.concatenate([q, o] + kv, 1))
    a_home, w_gate, w_up, w_down = lax.optimization_barrier((plain(jnp.stack(a_home)), w_gate, w_up, w_down))
    m_home = [
        jnp.concatenate(pieces, 1)
        for pieces in zip(quarters(w_gate[0]), quarters(w_up[0]), quarters(w_down[0].T))
    ]
    homes = {
        "a": a_home,
        "m0": plain(jnp.stack([value[: rb // 2] for value in m_home])),
        "m1": plain(jnp.stack([value[rb // 2 :] for value in m_home])),
    }

    def rolled(value):
        half = value.shape[-1] // 2
        return jnp.where(h == 0, value, jnp.concatenate([value[..., half:], value[..., :half]], -1))

    def fetch(name):
        clock.add(name, *FETCH[name], lambda: homes[name], to_groups)

    def spread(name):
        i, layer = int(name[1]), int(name[2])
        source, block = ("a", i) if name[0] == "a" else (f"m{i % 2}", i // 2)
        plan = SPREAD[name]

        def start():
            return clock.ready[source][2 * layer + block]

        def onward():
            value = [start(), clock.ready[name + "h"]]
            if groups > 1:
                value = [lax.all_gather(half, "g", axis=0, tiled=True) for half in value]
            clock.ready[name] = jnp.concatenate(value)
            return clock.ready[name]

        clock.add(name + "h", plan[0], plan[1], start, lambda value: swap(value, "h"))
        clock.add(name + "y", plan[2], plan[3], onward, lambda value: swap(value, "y"))

    def places_of(kind):
        count = 2 if kind == "m" else 1
        size = rb // count
        for i in range(4 * groups):
            half, block, group = i // (2 * groups), i // groups % 2, i % groups
            for j in range(count):
                yield block * count + j, (half * groups + group) * size, size

    def weight(kind, layer):
        return [
            jnp.concatenate(
                [
                    clock.ready[f"{kind}{part}{layer}{step}"][low : low + size]
                    for part, low, size in places_of(kind)
                ]
            )
            for step in ("", "y")
        ]

    for name in FETCH:
        fetch(name)
    for name in SPREAD:
        spread(name)

    rows, packed = clock.point("in", (rows, packed))
    own_rows = take(rows, h)
    other_rows = swap(take(rows, 1 - h), "h")
    keep = jnp.where(s == h, own_rows, other_rows)
    passed = swap(jnp.where(s == h, other_rows, own_rows), "s")
    entering = jnp.where(s == 0, keep, passed)
    cotangent = rolled(jnp.where(s == 0, passed, keep))
    entering = rolled(entering)
    packed = pair(k, packed, swap(packed, "k"), 1)
    packed = pair(s, packed, swap(packed, "s"))
    packed = pair(y, packed, swap(packed, "y"), 1).reshape(2, cols, -1).astype(f32)
    gain_a = rolled(packed[:, :, :width].reshape(2, model))
    gain_m = rolled(packed[:, :, width : 2 * width].reshape(2, model))
    gain_q = packed[:, 0, 2 * width : 2 * width + head]
    gain_k = packed[:, 0, 2 * width + head :]

    segments = take(segment_ids, 2 * y + h)
    part = tok // 2
    slots = slots_of(s, t, k, g, groups, part)
    first_run = jnp.sum((segments == 0).astype(jnp.int32))
    filled = jnp.sum((segments >= 0).astype(jnp.int32))

    def segments_at(places):
        return jnp.where(places < first_run, 0, jnp.where(places < filled, 1, -1))

    my_segments = segments_at(slots)
    offsets = slots - jnp.where(slots < first_run, 0, jnp.where(slots < filled, first_run, filled))
    inv_freq = THETA ** (-jnp.arange(0, head, 2, dtype=f32) / head)
    angles = offsets.astype(f32)[:, None] * inv_freq[None, :]
    cosine = jnp.concatenate([jnp.cos(angles)] * 2, 1)
    sine = jnp.concatenate([jnp.sin(angles)] * 2, 1)
    valid = (my_segments[:part] >= 0).astype(f32)
    key_slots = lax.all_gather(slots, "g", axis=0, tiled=True) if groups > 1 else slots
    key_segments = segments_at(key_slots)
    allowed = (my_segments[:, None] == key_segments[None, :]) & (
        key_slots[None, :] <= slots[:, None]
    )

    def all_keys(value):
        return lax.all_gather(value, "g", axis=0, tiled=True) if groups > 1 else value

    def sum_keys(value):
        if groups > 1:
            return lax.psum_scatter(value.astype(bf16), "g", scatter_dimension=0, tiled=True).astype(f32)
        return value

    def scores_of(q, keys):
        scores = jnp.einsum("qhd,khd->hqk", q, keys, preferred_element_type=f32) * scale_qk
        return jnp.where(allowed[None], scores, -1e30)

    entering, cotangent = clock.point("rows", (entering, cotangent))
    top = cotangent.astype(f32) * valid[:, None]
    kept = {}

    def forward(layer, residual):
        def at(place):
            return lambda chain: clock.point(f"F{layer}{place}", chain)

        scale_a = rms(residual)
        normed = (residual * scale_a * gain_a[layer]).astype(bf16)
        xa = at(2)(gather_tokens(at(0)(normed), at(1)))
        if layer == 0:
            for label in ("c1", "c2", "c3"):
                xa = clock.point(label, xa)
        wa = weight("a", layer)
        q_raw = jnp.stack([dot(xa, w[:, :head]) for w in wa], 1)
        raw = jnp.stack([dot(xa, w[:, 2 * head :]) for w in wa], 1)
        k_raw = raw[:, :, :head]
        v = raw[:, :, head:].astype(bf16)
        q = rotate(q_raw, gain_q[layer], cosine, sine).astype(bf16)
        keys = rotate(k_raw, gain_k[layer], cosine, sine).astype(bf16)
        keys, values = all_keys(keys), all_keys(v)
        scores = scores_of(q, keys)
        peak = jnp.max(scores, axis=2, keepdims=True)
        exps = jnp.exp(scores - peak)
        denom = jnp.sum(exps, axis=2, keepdims=True)
        mixing = (exps / denom).astype(bf16)
        lse = peak + jnp.log(denom)
        o = jnp.einsum("hqk,khd->qhd", mixing, values, preferred_element_type=f32)
        o = o.astype(bf16)
        near, far = at(3)(split_product((o[:, 0], o[:, 1]), [w[:, head : 2 * head] for w in wa]))
        middle = at(5)(residual + scatter_sum(near, far, at(4)))
        scale_m = rms(middle)
        normed = (middle * scale_m * gain_m[layer]).astype(bf16)
        xm = at(7)(gather_tokens(normed, at(6)))
        if layer == 0:
            xm, grad = lax.optimization_barrier((xm, top.astype(bf16)))
            xm, kept["g3"] = lax.optimization_barrier((xm, gather_tokens(grad, lambda value: value)))
        wm = weight("m", layer)
        hidden = []
        for w in wm:
            both = dot(xm, w[:, : 2 * ff])
            hidden.append((both[:, :ff], both[:, ff:]))
        act = [(gate * jax.nn.sigmoid(gate) * up).astype(bf16) for gate, up in hidden]
        kept[layer] = (residual, scale_a, xa, q_raw, k_raw, q, keys, values, lse, o, middle, scale_m, xm, hidden, act, wa, wm)

    def project(layer, act):
        return split_product(act, [w[:, 2 * ff :] for w in kept[layer][-1]])

    partial = {}

    def back(name):
        plan = RETURN[name]
        part, layer = int(name[1]), name[2]

        def rows_of(i):
            value = partial[name[0] + layer][i]
            rows = rb // (2 if name[0] == "m" else 1)
            lows = [
                j * rows for j, (index, _, _) in enumerate(places_of(name[0])) if index == part
            ]
            return jnp.concatenate([value[low : low + rows] for low in lows])

        def onward():
            total = rows_of(0).astype(f32) + clock.ready["back_y" + name].astype(f32)
            count = total.shape[0] // 2
            mine, other = total[:count], total[count:]
            if groups > 1:
                mine, other = (
                    lax.psum_scatter(half.astype(bf16), "g", scatter_dimension=0, tiled=True)
                    for half in (mine, other)
                )
            partial["sum" + name] = mine.astype(bf16)
            return other.astype(bf16)

        clock.add("back_y" + name, plan[0], plan[1], lambda: rows_of(1), lambda value: swap(value, "y"))
        clock.add("back_h" + name, plan[2], plan[3], onward, lambda value: swap(value, "h"))

    def summed(name):
        return (partial["sum" + name].astype(f32) + clock.ready["back_h" + name].astype(f32)).astype(bf16)

    def both_layers(name):
        names = ("a0", "a1") if name == "a" else (name, f"m{int(name[1]) + 2}")
        return plain(jnp.stack([summed(f"{part}{layer}") for layer in (0, 1) for part in names]))

    for name in RETURN:
        back(name)
    for name, plan in HOME.items():
        clock.add("home" + name, *plan, lambda name=name: both_layers(name), to_groups)

    def backward(layer, grad_top, g3):
        def at(place):
            return lambda chain: clock.point(f"B{layer}{place}", chain)

        (
            residual, scale_a, xa, q_raw, k_raw, q, keys, values, lse, o, middle, scale_m, xm, hidden,
            act, wa, wm,
        ) = kept[layer]
        d_act = [dot(g3, w[:, 2 * ff :]) for w in wm]
        d_hidden = []
        for grad, (gate, up) in zip(d_act, hidden):
            sig = jax.nn.sigmoid(gate)
            d_gate = (grad * up * sig * (1 + gate * (1 - sig))).astype(bf16)
            d_up = (grad * gate * sig).astype(bf16)
            d_hidden.append(jnp.concatenate([d_gate, d_up], 1))
        near, far = split_product(d_hidden, [w[:, : 2 * ff] for w in wm])
        partial[f"m{layer}"] = [
            plain(jnp.concatenate([t_dot(xm, d).astype(bf16), t_dot(g3, a).astype(bf16)], 1))
            for d, a in zip(d_hidden, act)
        ]
        near, far = at(3)((near, far))
        def after_core(chain):
            chain, partial[f"m{layer}"] = lax.optimization_barrier((chain, partial[f"m{layer}"]))
            return at(4)(chain)

        d_xm = at(5)(scatter_sum(near, far, after_core))
        d_mid, d_gain_m = norm_back(middle, scale_m, gain_m[layer], d_xm)
        d_mid = grad_top + d_mid
        g2 = at(7)(gather_tokens(d_mid.astype(bf16), at(6)))
        d_o = jnp.stack([dot(g2, w[:, head : 2 * head]).astype(bf16) for w in wa], 1)
        mixing = jnp.exp(scores_of(q, keys) - lse)
        d_mix = jnp.einsum("qhd,khd->hqk", d_o, values, preferred_element_type=f32)
        inner = jnp.sum(mixing * d_mix, axis=2, keepdims=True)
        d_scores = (mixing * (d_mix - inner)).astype(bf16)
        d_q = jnp.einsum("hqk,khd->qhd", d_scores, keys, preferred_element_type=f32) * scale_qk
        d_k = jnp.einsum("hqk,qhd->khd", d_scores, q, preferred_element_type=f32) * scale_qk
        d_v = jnp.einsum("hqk,qhd->khd", mixing.astype(bf16), d_o, preferred_element_type=f32)
        d_k, d_v = sum_keys(d_k), sum_keys(d_v)
        _, pull_q = jax.vjp(lambda raw, gain: rotate(raw, gain, cosine, sine), q_raw, gain_q[layer])
        _, pull_k = jax.vjp(lambda raw, gain: rotate(raw, gain, cosine, sine), k_raw, gain_k[layer])
        d_q_raw, d_gain_q = pull_q(d_q)
        d_k_raw, d_gain_k = pull_k(d_k)
        d_q_raw, d_kv_raw = d_q_raw.astype(bf16), jnp.concatenate([d_k_raw, d_v], 2).astype(bf16)
        d_raw = [d_q_raw[:, 0], d_q_raw[:, 1], d_kv_raw[:, 0], d_kv_raw[:, 1]]
        near, far = at(8)(split_product(d_raw, [w[:, :head] for w in wa] + [w[:, 2 * head :] for w in wa]))
        partial[f"a{layer}"] = [
            plain(
                jnp.concatenate(
                    [
                        value.astype(bf16)
                        for value in (t_dot(xa, d_q_raw[:, i]), t_dot(g2, o[:, i]), t_dot(xa, d_kv_raw[:, i]))
                    ],
                    1,
                )
            )
            for i in (0, 1)
        ]
        d_xa = scatter_sum(near, far, at(9))
        d_res, d_gain_a = norm_back(residual, scale_a, gain_a[layer], d_xa)
        return d_mid + d_res, (d_gain_a, d_gain_m, d_gain_q, d_gain_k)

    forward(0, entering.astype(f32))
    act = kept[0][14]
    near, far = clock.point("F09", project(0, act))
    middle = kept[0][10] + scatter_sum(near, far, lambda value: value)
    forward(1, middle.astype(bf16).astype(f32))
    grad, gains1 = backward(1, top, kept["g3"])
    grad = clock.point("B00", grad.astype(bf16))
    g3 = clock.point("B02", gather_tokens(grad, lambda value: clock.point("B01", value)))
    grad, gains0 = backward(0, grad.astype(f32), g3)
    grad = clock.point("E0", grad)

    act, grad = lax.optimization_barrier((kept[1][14], grad))
    near, far = project(1, act)
    sums = []
    for gains in (gains0, gains1):
        sums += [rolled(gains[0]), rolled(gains[1]), gains[2], gains[3]]
    sums = jnp.concatenate(sums).reshape(2, -1)
    sums = sums + swap(sums, "k")
    output = kept[1][10] + scatter_sum(near, far, lambda value: value)

    grad, output, sums = clock.point("E1", (grad, output, sums))
    low, high = rolled(grad.astype(bf16)), rolled(output.astype(bf16))
    keep = jnp.where(s == 0, low, high)
    passed = swap(jnp.where(s == 0, high, low), "s")
    sums = sums + swap(sums, "y")
    sums = sums + swap(sums, "t")
    mine = jnp.where(s == h, keep, passed)
    other = swap(jnp.where(s == h, passed, keep), "h")
    mine, other, sums = clock.point("E2", (mine, other, sums))
    mine, other, sums = clock.point("E3", (mine, other, sums))
    rows = pair(h, mine, other).reshape(2, tok // 2, cols, width).transpose(2, 0, 1, 3)
    rows = exchange(rows, ("y", "k"))
    sums = sums + swap(sums, "s")
    sums = sums + swap(sums, "h")
    rows = rows.reshape(2, 2, 2, tok // 2, width).transpose(0, 2, 1, 3, 4)
    section_out = rows.reshape(micro, tok, width)
    if groups > 1:
        sums = lax.psum(sums, "g")
    sums = take(sums, s)

    def columns(value):
        return jnp.concatenate([value[i] for i in range(4)], 1).astype(f32)

    full_a = to_groups(both_layers("a"))
    full_m = jnp.concatenate([clock.ready["homem0"], clock.ready["homem1"]], 1)
    full_gate, full_up = columns(full_m[..., :ff]), columns(full_m[..., ff : 2 * ff])
    full_down = columns(full_m[..., 2 * ff :]).T
    full_q = columns(full_a[..., :head])
    full_out = columns(full_a[..., head : 2 * head]).T
    full_kv = full_a[..., 2 * head :].astype(f32)
    full_kv = [full_kv[0] + full_kv[1], full_kv[2] + full_kv[3]]
    full_k, full_v = (
        jnp.concatenate([half[:, i * head : (i + 1) * head] for half in full_kv], 1) for i in (0, 1)
    )
    return (
        section_out.astype(f32)[None],
        full_q[None],
        full_k[None],
        full_v[None],
        full_out[None],
        full_gate[None],
        full_up[None],
        full_down[None],
        sums[None, :model],
        sums[None, model : 2 * model],
        sums[None, 2 * model : 2 * model + head],
        sums[None, 2 * model + head :],
    )


def solution(mesh):
    sections, row_count, col_count = (mesh.shape[name] for name in ("section", "row", "col"))
    shape = (sections, 2, 2, row_count // 4, 2, col_count // 2)
    mesh = Mesh(np.asarray(mesh.devices).reshape(shape), ("s", "h", "t", "g", "y", "k"))
    row, col = ("h", "t", "g"), ("y", "k")
    in_row, in_col = P("s", row, col), P("s", col, row)
    return jax.shard_map(
        body,
        mesh=mesh,
        in_specs=(
            P("s", None, row, col), P(), in_row, in_row, in_row, in_col, in_row, in_row, in_col,
            P("s", col), P("s", col), P("s", None), P("s", None),
        ),
        out_specs=(
            P("s", None, row, col), in_row, in_row, in_row, in_col, in_row, in_row, in_col,
            P("s", None), P("s", None), P("s", None), P("s", None),
        ),
        check_vma=False,
    )
```

```python
import jax
import jax.numpy as jnp
import numpy as np
from jax import lax
from jax.experimental.layout import Layout, with_layout_constraint
from jax.sharding import Mesh
from jax.sharding import PartitionSpec as P

EPS = 1e-06
THETA = 1000000.0
f32 = jnp.float32
bf16 = jnp.bfloat16


def swap(value, axis):
    return lax.ppermute(value, axis, [(0, 1), (1, 0)])


def exchange(value, axes):
    return lax.all_to_all(value, axes, 0, 0, tiled=True)


def take(value, index, axis=0):
    return lax.dynamic_index_in_dim(value, index, axis, keepdims=False)


def pair(bit, mine, other, axis=0):
    low = jnp.where(bit == 0, mine, other)
    high = jnp.where(bit == 0, other, mine)
    return jnp.stack([low, high], axis)


def plain(value):
    return with_layout_constraint(value, Layout(major_to_minor=tuple(range(value.ndim))))


def dot(left, right):
    return jnp.dot(left, right, preferred_element_type=f32)


def dot_t(left, right):
    return lax.dot_general(left, right, (((1,), (1,)), ((), ())), preferred_element_type=f32)


def t_dot(left, right):
    return lax.dot_general(left, right, (((0,), (0,)), ((), ())), preferred_element_type=f32)


def cross(value):
    return lax.ppermute(value, ("s", "t"), [(i, 3 - i) for i in range(4)])


def gather_near(mine):
    return [mine, swap(mine, "s"), swap(mine, "t"), cross(mine)]


def gather_core(pieces):
    core = jnp.concatenate(pieces)
    return jnp.concatenate([core, swap(core, "k")])


def gather_tokens(mine, middle):
    return gather_core(middle(gather_near(mine)))


def slots_of(s, t, k, g, groups, part):
    pieces = []
    for dk in (0, 1):
        for ds, dt in ((0, 0), (1, 0), (0, 1), (1, 1)):
            block = ((s ^ ds) * 2 + (t ^ dt)) * groups + g
            start = block * (2 * part) + (k ^ dk) * part
            pieces.append(start + jnp.arange(part, dtype=jnp.int32))
    return jnp.concatenate(pieces)


def scatter_sum(near, far, middle, last):
    total = near + swap(far, "k").astype(f32)
    part = total.shape[0] // 4
    total, far = middle((total[:part], total[part:].astype(bf16)))
    pieces = [swap(far[:part], "s"), swap(far[part : 2 * part], "t"), cross(far[2 * part :])]
    total, pieces = last((total, pieces))
    return total + sum(piece.astype(f32) for piece in pieces)


def split_product(lefts, rights):
    half = lefts[0].shape[0] // 2
    far = sum(dot_t(left[half:], right) for left, right in zip(lefts, rights)).astype(bf16)
    near = sum(dot_t(left[:half], right) for left, right in zip(lefts, rights))
    return near, far


class Clock:
    def __init__(self):
        self.plans, self.flying, self.ready, self.loose = {}, {}, {}, {}

    def add(self, name, begin, end, make, send):
        self.plans[name] = (begin, end, make, send)

    def split(self, name, value):
        self.ready[name] = [value[i] for i in range(value.shape[0])]
        self.loose[name] = self.ready[name]

    def point(self, label, chain):
        ends = [name for name, plan in self.plans.items() if plan[1] == label]
        if ends or self.loose:
            flying = [self.flying[name] for name in ends]
            chain, arrived, loose = lax.optimization_barrier((chain, flying, self.loose))
            self.ready.update(loose)
            self.loose = {}
            for name, value in zip(ends, arrived):
                if name in FETCH or name == "a":
                    self.split(name, value)
                else:
                    self.ready[name] = value
        begins = [name for name, plan in self.plans.items() if plan[0] == label]
        if begins:
            values = [self.plans[name][2]() for name in begins]
            passed, values = lax.optimization_barrier((chain, values))
            if label[0] == "E":
                chain = passed
            for name, value in zip(begins, values):
                self.flying[name] = self.plans[name][3](value)
        return chain


def rms(residual):
    return lax.rsqrt(jnp.mean(residual * residual, axis=1, keepdims=True) + EPS)


def norm_back(residual, scale, gain, grad):
    lifted = grad * gain
    inner = jnp.mean(lifted * residual, axis=1, keepdims=True)
    grad_residual = scale * lifted - residual * (scale**3 * inner)
    return grad_residual, jnp.sum(grad * residual * scale, axis=0)


def rotate(raw, gain, cosine, sine):
    scaled = raw * lax.rsqrt(jnp.mean(raw * raw, axis=2, keepdims=True) + EPS) * gain
    half = raw.shape[2] // 2
    turned = jnp.concatenate([-scaled[:, :, half:], scaled[:, :, :half]], axis=2)
    return scaled * cosine[:, None, :] + turned * sine[:, None, :]


FETCH = {
    "m0": ("F01", "c1"),
    "m1": ("c1", "F03"),
}
SPREAD = {
    "a00": ("p0", "F01", "F01", "c1"),
    "a10": ("F01", "c1", "c1", "c2"),
    "m00": ("c1", "c2", "c2", "F03"),
    "m20": ("c2", "F03", "F03", "F05"),
    "m10": ("F03", "F05", "F05", "F06"),
    "m30": ("F05", "F06", "F06", "F07"),
    "a01": ("F06", "F07", "F07", "F09"),
    "a11": ("F07", "F09", "F09", "F10"),
    "m01": ("F09", "F10", "F10", "F11"),
    "m21": ("F10", "F11", "F11", "F13"),
    "m11": ("F11", "F13", "F13", "F15"),
    "m31": ("F13", "F15", "F15", "F16"),
}
RETURN = {
    "m01": ("B12", "B13", "B13", "B15"),
    "m21": ("B13", "B15", "B15", "B16"),
    "m11": ("B15", "B16", "B16", "B18"),
    "m31": ("B16", "B18", "B18", "B1X"),
    "a01": ("B18", "B1X", "B1X", "B01"),
    "a11": ("B1X", "B01", "B01", "B02"),
    "m00": ("B02", "B04", "B04", "B05"),
    "m20": ("B04", "B05", "B05", "B06"),
    "m10": ("B05", "B06", "B06", "B08"),
    "m30": ("B06", "B08", "B08", "B0X"),
    "a00": ("B08", "B0X", "B0X", "E1"),
    "a10": ("B0X", "E1", "E1", "E2"),
}
HOME = {
    "m0": ("B06", "B0X"),
    "m1": ("B0X", "E2"),
}


def body(
    boundary, segment_ids, w_query, key_projection, value_projection, w_out, w_gate, w_up, w_down,
    attn_gain, mlp_gain, query_gain, key_norm_gain,
):
    s, h, t, g, y, k = (lax.axis_index(name) for name in ("s", "h", "t", "g", "y", "k"))
    groups = lax.axis_size("g")
    micro, tok, width = boundary.shape[1:]
    cols = lax.axis_size("y") * lax.axis_size("k")
    model = width * cols
    head = query_gain.shape[1]
    span = segment_ids.shape[1]
    rb = w_query.shape[1]
    ff = w_gate.shape[2] // 4
    scale_qk = head ** (-0.5)
    clock = Clock()

    packed = jnp.concatenate([attn_gain[0], mlp_gain[0], query_gain[0], key_norm_gain[0]])[None]
    packed = pair(s, packed, swap(packed, "s"))

    segments = take(segment_ids, 2 * y + h)
    part = tok // 2
    slots = slots_of(s, t, k, g, groups, part)
    first_run = jnp.sum((segments == 0).astype(jnp.int32))
    filled = jnp.sum((segments >= 0).astype(jnp.int32))

    def segments_at(places):
        return jnp.where(places < first_run, 0, jnp.where(places < filled, 1, -1))

    my_segments = segments_at(slots)
    offsets = slots - jnp.where(slots < first_run, 0, jnp.where(slots < filled, first_run, filled))
    inv_freq = THETA ** (-jnp.arange(0, head, 2, dtype=f32) / head)
    angles = offsets.astype(f32)[:, None] * inv_freq[None, :]
    cosine = jnp.concatenate([jnp.cos(angles)] * 2, 1)
    sine = jnp.concatenate([jnp.sin(angles)] * 2, 1)
    valid = (my_segments[:part] >= 0).astype(f32)
    key_slots = lax.all_gather(slots, "g", axis=0, tiled=True) if groups > 1 else slots
    key_segments = segments_at(key_slots)
    allowed = (my_segments[:, None] == key_segments[None, :]) & (
        key_slots[None, :] <= slots[:, None]
    )

    rows = boundary[0].reshape(2, 2 * tok, width)
    rows = pair(y, take(rows, y), swap(take(rows, 1 - y), "y")).reshape(2, 2, 2, tok // 2, width)
    rows = pair(k, take(rows, k, 2), swap(take(rows, 1 - k, 2), "k"))
    rows = jnp.stack(
        [jnp.concatenate([rows[j, i, m] for i in (0, 1) for j in (0, 1)], 1) for m in (0, 1)]
    )

    def quarters(weight):
        size = weight.shape[1] // 4
        return [weight[:, i * size : (i + 1) * size] for i in range(4)]

    def to_groups(value):
        return exchange(value, ("s", "t"))

    a_home = []
    for i, (q, o) in enumerate(zip(quarters(w_query[0]), quarters(w_out[0].T))):
        low = (i // 2) * head
        kv = [w[0, :, low : low + head] for w in (key_projection, value_projection)]
        a_home.append(jnp.concatenate([q, o] + kv, 1))
    a_home, packed = lax.optimization_barrier((plain(jnp.stack(a_home)), packed))
    fetched_a = to_groups(a_home)
    def rolled(value):
        half = value.shape[-1] // 2
        return jnp.where(h == 0, value, jnp.concatenate([value[..., half:], value[..., :half]], -1))

    homes = {}

    def fetch(name):
        clock.add(name, *FETCH[name], lambda: homes[name], to_groups)

    def spread(name):
        i, layer = int(name[1]), int(name[2])
        source, block = ("a", i) if name[0] == "a" else (f"m{i % 2}", i // 2)
        plan = SPREAD[name]

        def start():
            return clock.ready[source][2 * layer + block]

        def onward():
            value = [start(), clock.ready[name + "h"]]
            if groups > 1:
                value = [lax.all_gather(half, "g", axis=0, tiled=True) for half in value]
            clock.ready[name] = jnp.concatenate(value)
            return clock.ready[name]

        clock.add(name + "h", plan[0], plan[1], start, lambda value: swap(value, "h"))
        clock.add(name + "y", plan[2], plan[3], onward, lambda value: swap(value, "y"))

    def places_of(kind):
        count = 2 if kind == "m" else 1
        size = rb // count
        for i in range(4 * groups):
            half, block, group = i // (2 * groups), i // groups % 2, i % groups
            for j in range(count):
                yield block * count + j, (half * groups + group) * size, size

    def weight(kind, layer):
        return [
            jnp.concatenate(
                [
                    clock.ready[f"{kind}{part}{layer}{step}"][low : low + size]
                    for part, low, size in places_of(kind)
                ]
            )
            for step in ("", "y")
        ]

    for name in FETCH:
        fetch(name)
    for name in SPREAD:
        spread(name)

    rows, w_gate, w_up, w_down = lax.optimization_barrier((rows, w_gate, w_up, w_down))
    m_home = [
        jnp.concatenate(pieces, 1)
        for pieces in zip(quarters(w_gate[0]), quarters(w_up[0]), quarters(w_down[0].T))
    ]
    homes.update({
        "m0": plain(jnp.stack([value[: rb // 2] for value in m_home])),
        "m1": plain(jnp.stack([value[rb // 2 :] for value in m_home])),
    })

    own_rows = take(rows, h)
    other_rows = swap(take(rows, 1 - h), "h")
    keep = jnp.where(s == h, own_rows, other_rows)
    passed = jnp.where(s == h, other_rows, own_rows)
    passed = swap(passed, "s")
    entering = rolled(jnp.where(s == 0, keep, passed))
    cotangent = rolled(jnp.where(s == 0, passed, keep))
    packed = pair(k, packed, swap(packed, "k"), 1)
    packed = pair(y, packed, swap(packed, "y"), 1).reshape(2, cols, -1).astype(f32)
    gain_a = rolled(packed[:, :, :width].reshape(2, model))
    gain_m = rolled(packed[:, :, width : 2 * width].reshape(2, model))
    gain_q = packed[:, 0, 2 * width : 2 * width + head]
    gain_k = packed[:, 0, 2 * width + head :]
    clock.flying["a"] = fetched_a
    clock.plans["a"] = (None, "p0", None, None)
    entering, cotangent, gain_a, gain_m, homes["m0"], homes["m1"] = clock.point(
        "p0", (entering, cotangent, gain_a, gain_m, homes["m0"], homes["m1"])
    )
    top = cotangent.astype(f32) * valid[:, None]
    kept = {}

    def all_keys(value):
        return lax.all_gather(value, "g", axis=0, tiled=True) if groups > 1 else value

    def sum_keys(value):
        if groups > 1:
            return lax.psum_scatter(value.astype(bf16), "g", scatter_dimension=0, tiled=True).astype(f32)
        return value

    def scores_of(q, keys):
        scores = jnp.einsum("qhd,khd->hqk", q, keys, preferred_element_type=f32) * scale_qk
        return jnp.where(allowed[None], scores, -1e30)

    def forward(layer, residual):
        def at(place):
            return lambda chain: clock.point(f"F{layer}{place}", chain)

        scale_a = rms(residual)
        normed = (residual * scale_a * gain_a[layer]).astype(bf16)
        def head_start(pieces):
            pieces = at(1)(pieces)
            if layer == 0:
                for label in ("c1", "c2"):
                    pieces = clock.point(label, pieces)
            return pieces

        xa = at(2)(gather_tokens(normed, head_start))
        wa = weight("a", layer)
        q_raw = jnp.stack([dot(xa, w[:, :head]) for w in wa], 1)
        raw = jnp.stack([dot(xa, w[:, 2 * head :]) for w in wa], 1)
        k_raw = raw[:, :, :head]
        v = raw[:, :, head:].astype(bf16)
        q = rotate(q_raw, gain_q[layer], cosine, sine).astype(bf16)
        keys = rotate(k_raw, gain_k[layer], cosine, sine).astype(bf16)
        keys, values = all_keys(keys), all_keys(v)
        scores = scores_of(q, keys)
        peak = jnp.max(scores, axis=2, keepdims=True)
        exps = jnp.exp(scores - peak)
        denom = jnp.sum(exps, axis=2, keepdims=True)
        mixing = (exps / denom).astype(bf16)
        lse = peak + jnp.log(denom)
        o = jnp.einsum("hqk,khd->qhd", mixing, values, preferred_element_type=f32)
        o = o.astype(bf16)
        near, far = at(3)(split_product((o[:, 0], o[:, 1]), [w[:, head : 2 * head] for w in wa]))
        middle = residual + scatter_sum(near, far, at(4), at(5))
        scale_m = rms(middle)
        normed = (middle * scale_m * gain_m[layer]).astype(bf16)
        xm = gather_tokens(normed, at(6))
        if layer == 1:
            xm, pieces = lax.optimization_barrier((xm, kept["g3"]))
            xm, kept["g3"] = lax.optimization_barrier((xm, gather_core(pieces)))
        xm = at(7)(xm)
        if layer == 0:
            xm, grad = lax.optimization_barrier((xm, top.astype(bf16)))
            kept["g3"] = gather_near(grad)
        wm = weight("m", layer)
        hidden = []
        for w in wm:
            both = dot(xm, w[:, : 2 * ff])
            hidden.append((both[:, :ff], both[:, ff:]))
        act = [(gate * jax.nn.sigmoid(gate) * up).astype(bf16) for gate, up in hidden]
        kept[layer] = (residual, scale_a, xa, q_raw, k_raw, q, keys, values, lse, o, middle, scale_m, xm, hidden, act, wa, wm)

    def project(layer, act):
        return split_product(act, [w[:, 2 * ff :] for w in kept[layer][-1]])

    partial = {}

    def back(name):
        plan = RETURN[name]
        part, layer = int(name[1]), name[2]

        def rows_of(i):
            rows = rb // (2 if name[0] == "m" else 1)
            lows = [j * rows for j, (index, _, _) in enumerate(places_of(name[0])) if index == part]
            return [
                t_dot(jnp.concatenate([left[:, low : low + rows] for low in lows], 1), right)
                for left, right in partial[name[0] + layer][i]
            ]

        def other():
            return plain(jnp.concatenate([value.astype(bf16) for value in rows_of(1)], 1))

        def onward():
            total, low = [], 0
            for value in rows_of(0):
                high = low + value.shape[1]
                total.append((value + clock.ready["back_y" + name][:, low:high].astype(f32)).astype(bf16))
                low = high
            total = plain(jnp.concatenate(total, 1))
            count = total.shape[0] // 2
            mine, other = total[:count], total[count:]
            if groups > 1:
                mine, other = (
                    lax.psum_scatter(half, "g", scatter_dimension=0, tiled=True) for half in (mine, other)
                )
            partial["sum" + name] = mine
            return other

        clock.add("back_y" + name, plan[0], plan[1], other, lambda value: swap(value, "y"))
        clock.add("back_h" + name, plan[2], plan[3], onward, lambda value: swap(value, "h"))

    def summed(name):
        return (partial["sum" + name].astype(f32) + clock.ready["back_h" + name].astype(f32)).astype(bf16)

    def both_layers(name):
        names = ("a0", "a1") if name == "a" else (name, f"m{int(name[1]) + 2}")
        return plain(jnp.stack([summed(f"{part}{layer}") for layer in (0, 1) for part in names]))

    for name in RETURN:
        back(name)
    for name, plan in HOME.items():
        clock.add("home" + name, *plan, lambda name=name: both_layers(name), to_groups)

    def backward(layer, grad_top, g3):
        def at(place):
            return lambda chain: clock.point(f"B{layer}{place}", chain)

        (
            residual, scale_a, xa, q_raw, k_raw, q, keys, values, lse, o, middle, scale_m, xm, hidden,
            act, wa, wm,
        ) = kept[layer]
        d_act = [dot(g3, w[:, 2 * ff :]) for w in wm]
        d_hidden = []
        for grad, (gate, up) in zip(d_act, hidden):
            sig = jax.nn.sigmoid(gate)
            d_gate = (grad * up * sig * (1 + gate * (1 - sig))).astype(bf16)
            d_up = (grad * gate * sig).astype(bf16)
            d_hidden.append(jnp.concatenate([d_gate, d_up], 1))
        partial[f"m{layer}"] = [((xm, d), (g3, a)) for d, a in zip(d_hidden, act)]
        d_hidden = at(2)(d_hidden)
        near, far = split_product(d_hidden, [w[:, : 2 * ff] for w in wm])
        near, far = at(3)((near, far))
        d_xm = scatter_sum(near, far, at(4), at(5))
        d_mid, d_gain_m = norm_back(middle, scale_m, gain_m[layer], d_xm)
        d_mid = grad_top + d_mid
        g2 = at(7)(gather_tokens(d_mid.astype(bf16), at(6)))
        d_o = jnp.stack([dot(g2, w[:, head : 2 * head]).astype(bf16) for w in wa], 1)
        mixing = jnp.exp(scores_of(q, keys) - lse)
        d_mix = jnp.einsum("qhd,khd->hqk", d_o, values, preferred_element_type=f32)
        inner = jnp.sum(mixing * d_mix, axis=2, keepdims=True)
        d_scores = (mixing * (d_mix - inner)).astype(bf16)
        d_q = jnp.einsum("hqk,khd->qhd", d_scores, keys, preferred_element_type=f32) * scale_qk
        d_k = jnp.einsum("hqk,qhd->khd", d_scores, q, preferred_element_type=f32) * scale_qk
        d_v = jnp.einsum("hqk,qhd->khd", mixing.astype(bf16), d_o, preferred_element_type=f32)
        d_k, d_v = sum_keys(d_k), sum_keys(d_v)
        _, pull_q = jax.vjp(lambda raw, gain: rotate(raw, gain, cosine, sine), q_raw, gain_q[layer])
        _, pull_k = jax.vjp(lambda raw, gain: rotate(raw, gain, cosine, sine), k_raw, gain_k[layer])
        d_q_raw, d_gain_q = pull_q(d_q)
        d_k_raw, d_gain_k = pull_k(d_k)
        d_q_raw, d_kv_raw = d_q_raw.astype(bf16), jnp.concatenate([d_k_raw, d_v], 2).astype(bf16)
        d_raw = [d_q_raw[:, 0], d_q_raw[:, 1], d_kv_raw[:, 0], d_kv_raw[:, 1]]
        partial[f"a{layer}"] = [
            ((xa, d_q_raw[:, i]), (g2, o[:, i]), (xa, d_kv_raw[:, i])) for i in (0, 1)
        ]
        near, far = at(8)(split_product(d_raw, [w[:, :head] for w in wa] + [w[:, 2 * head :] for w in wa]))
        d_xa = scatter_sum(near, far, at(9), lambda value: clock.point(f"B{layer}X", value))
        d_res, d_gain_a = norm_back(residual, scale_a, gain_a[layer], d_xa)
        return d_mid + d_res, (d_gain_a, d_gain_m, d_gain_q, d_gain_k)

    forward(0, entering.astype(f32))
    act = kept[0][14]
    near, far, kept["g3"] = clock.point("F09", (*project(0, act), kept["g3"]))
    middle = kept[0][10] + scatter_sum(near, far, lambda value: value, lambda value: clock.point("F10", value))
    forward(1, middle.astype(bf16).astype(f32))
    grad, gains1 = backward(1, top, kept["g3"])
    grad = grad.astype(bf16)
    pieces = clock.point("B01", gather_near(grad))
    pieces, act = lax.optimization_barrier((pieces, kept[1][14]))
    near, far = project(1, act)
    output = kept[1][10] + scatter_sum(near, far, lambda value: value, lambda value: value)
    g3, kept["output"] = lax.optimization_barrier((gather_core(pieces), output))
    grad, gains0 = backward(0, grad.astype(f32), g3)

    low, high = rolled(grad.astype(bf16)), rolled(kept["output"].astype(bf16))
    keep = jnp.where(s == 0, low, high)
    passed = swap(jnp.where(s == 0, high, low), "s")
    (keep, passed), gains0, gains1 = clock.point("E1", ((keep, passed), gains0, gains1))
    sums = []
    for gains in (gains0, gains1):
        sums += [rolled(gains[0]), rolled(gains[1]), gains[2], gains[3]]
    sums = jnp.concatenate(sums)
    sums = sums.reshape(-1, head)
    sums = sums + swap(sums, "k")
    sums = sums + swap(sums, "t")
    keep, passed, sums = clock.point("E2", (keep, passed, sums))
    last = both_layers("a")
    ready = {name: clock.ready["home" + name] for name in HOME}
    last, keep, passed, sums, ready = lax.optimization_barrier((last, keep, passed, sums, ready))
    full_a = to_groups(last)
    mine = jnp.where(s == h, keep, passed)
    other = swap(jnp.where(s == h, passed, keep), "h")
    sums = sums + swap(sums, "y")
    rows = pair(h, mine, other)
    blocks = [jnp.stack([rows[..., (2 * i + j) * width : (2 * i + j + 1) * width] for i in (0, 1)]) for j in (0, 1)]
    mine, other = (jnp.where(k == j, blocks[0], blocks[1]) for j in (0, 1))
    rows = pair(k, mine, swap(other, "k"), 2).reshape(2, 2, tok, width)
    rows = pair(y, take(rows, y), swap(take(rows, 1 - y), "y"))
    section_out = rows.reshape(micro, tok, width)
    sums = sums + swap(sums, "s")
    sums = sums + swap(sums, "h")
    if groups > 1:
        sums = lax.psum(sums, "g")
    sums = take(sums.reshape(2, -1), s)

    def columns(value):
        return jnp.concatenate([value[i] for i in range(4)], 1).astype(f32)

    full_m = jnp.concatenate([ready["m0"], ready["m1"]], 1)
    full_gate, full_up = columns(full_m[..., :ff]), columns(full_m[..., ff : 2 * ff])
    full_down = columns(full_m[..., 2 * ff :]).T
    full_q = columns(full_a[..., :head])
    full_out = columns(full_a[..., head : 2 * head]).T
    full_kv = full_a[..., 2 * head :].astype(f32)
    full_kv = [full_kv[0] + full_kv[1], full_kv[2] + full_kv[3]]
    full_k, full_v = (
        jnp.concatenate([half[:, i * head : (i + 1) * head] for half in full_kv], 1) for i in (0, 1)
    )
    return (
        section_out.astype(f32)[None],
        full_q[None],
        full_k[None],
        full_v[None],
        full_out[None],
        full_gate[None],
        full_up[None],
        full_down[None],
        sums[None, :model],
        sums[None, model : 2 * model],
        sums[None, 2 * model : 2 * model + head],
        sums[None, 2 * model + head :],
    )


def solution(mesh):
    sections, row_count, col_count = (mesh.shape[name] for name in ("section", "row", "col"))
    shape = (sections, 2, 2, row_count // 4, 2, col_count // 2)
    mesh = Mesh(np.asarray(mesh.devices).reshape(shape), ("s", "h", "t", "g", "y", "k"))
    row, col = ("h", "t", "g"), ("y", "k")
    in_row, in_col = P("s", row, col), P("s", col, row)
    return jax.shard_map(
        body,
        mesh=mesh,
        in_specs=(
            P("s", None, row, col), P(), in_row, in_row, in_row, in_col, in_row, in_row, in_col,
            P("s", col), P("s", col), P("s", None), P("s", None),
        ),
        out_specs=(
            P("s", None, row, col), in_row, in_row, in_row, in_col, in_row, in_row, in_col,
            P("s", None), P("s", None), P("s", None), P("s", None),
        ),
        check_vma=False,
    )
```

```python
import jax
import jax.numpy as jnp
import numpy as np
from jax import lax
from jax.experimental.layout import Layout, with_layout_constraint
from jax.sharding import Mesh
from jax.sharding import PartitionSpec as P

EPS = 1e-06
THETA = 1000000.0
f32 = jnp.float32
bf16 = jnp.bfloat16


def swap(value, axis):
    return lax.ppermute(value, axis, [(0, 1), (1, 0)])


def exchange(value, axes):
    return lax.all_to_all(value, axes, 0, 0, tiled=True)


def take(value, index, axis=0):
    return lax.dynamic_index_in_dim(value, index, axis, keepdims=False)


def pair(bit, mine, other, axis=0):
    low = jnp.where(bit == 0, mine, other)
    high = jnp.where(bit == 0, other, mine)
    return jnp.stack([low, high], axis)


def plain(value):
    return with_layout_constraint(value, Layout(major_to_minor=tuple(range(value.ndim))))


def dot(left, right):
    return jnp.dot(left, right, preferred_element_type=f32)


def dot_t(left, right):
    return lax.dot_general(left, right, (((1,), (1,)), ((), ())), preferred_element_type=f32)


def t_dot(left, right):
    return lax.dot_general(left, right, (((0,), (0,)), ((), ())), preferred_element_type=f32)


def cross(value):
    return lax.ppermute(value, ("s", "t"), [(i, 3 - i) for i in range(4)])


def gather_near(mine):
    return [mine, swap(mine, "s"), swap(mine, "t"), cross(mine)]


def gather_core(pieces):
    core = jnp.concatenate(pieces)
    return jnp.concatenate([core, swap(core, "k")])


def gather_tokens(mine, middle):
    return gather_core(middle(gather_near(mine)))


def slots_of(s, t, k, g, groups, part):
    pieces = []
    for dk in (0, 1):
        for ds, dt in ((0, 0), (1, 0), (0, 1), (1, 1)):
            block = ((s ^ ds) * 2 + (t ^ dt)) * groups + g
            start = block * (2 * part) + (k ^ dk) * part
            pieces.append(start + jnp.arange(part, dtype=jnp.int32))
    return jnp.concatenate(pieces)


def scatter_core(near, far):
    total = near + swap(far, "k").astype(f32)
    part = total.shape[0] // 4
    return total[:part], total[part:].astype(bf16)


def scatter_near(total, far):
    part = total.shape[0]
    return total, [swap(far[:part], "s"), swap(far[part : 2 * part], "t"), cross(far[2 * part :])]


def added(total, pieces):
    return total + sum(piece.astype(f32) for piece in pieces)


def scatter_sum(near, far, middle, last):
    return added(*last(scatter_near(*middle(scatter_core(near, far)))))


def split_product(lefts, rights):
    half = lefts[0].shape[0] // 2
    far = sum(dot_t(left[half:], right) for left, right in zip(lefts, rights)).astype(bf16)
    near = sum(dot_t(left[:half], right) for left, right in zip(lefts, rights))
    return near, far


class Clock:
    def __init__(self):
        self.plans, self.flying, self.ready, self.loose = {}, {}, {}, {}

    def add(self, name, begin, end, make, send):
        self.plans[name] = (begin, end, make, send)

    def split(self, name, value):
        self.ready[name] = [value[i] for i in range(value.shape[0])]
        self.loose[name] = self.ready[name]

    def point(self, label, chain):
        ends = [name for name, plan in self.plans.items() if plan[1] == label]
        if ends or self.loose:
            flying = [self.flying[name] for name in ends]
            chain, arrived, loose = lax.optimization_barrier((chain, flying, self.loose))
            self.ready.update(loose)
            self.loose = {}
            for name, value in zip(ends, arrived):
                if name in FETCH or name == "a":
                    self.split(name, value)
                else:
                    self.ready[name] = value
        begins = [name for name, plan in self.plans.items() if plan[0] == label]
        if begins:
            values = [self.plans[name][2]() for name in begins]
            passed, values = lax.optimization_barrier((chain, values))
            if label[0] == "E":
                chain = passed
            for name, value in zip(begins, values):
                self.flying[name] = self.plans[name][3](value)
        return chain


def rms(residual):
    return lax.rsqrt(jnp.mean(residual * residual, axis=1, keepdims=True) + EPS)


def norm_back(residual, scale, gain, grad):
    lifted = grad * gain
    inner = jnp.mean(lifted * residual, axis=1, keepdims=True)
    grad_residual = scale * lifted - residual * (scale**3 * inner)
    return grad_residual, jnp.sum(grad * residual * scale, axis=0)


def rotate(raw, gain, cosine, sine):
    scaled = raw * lax.rsqrt(jnp.mean(raw * raw, axis=2, keepdims=True) + EPS) * gain
    half = raw.shape[2] // 2
    turned = jnp.concatenate([-scaled[:, :, half:], scaled[:, :, :half]], axis=2)
    return scaled * cosine[:, None, :] + turned * sine[:, None, :]


FETCH = {
    "m0": ("F01", "c1"),
    "m1": ("c1", "F03"),
}
SPREAD = {
    "a00": ("p0", "F01", "F01", "c1"),
    "a10": ("F01", "c1", "c1", "c2"),
    "m00": ("c1", "c2", "c2", "F03"),
    "m20": ("c2", "F03", "F03", "F05"),
    "m10": ("F03", "F05", "F05", "F06"),
    "m30": ("F05", "F06", "F06", "F07"),
    "a01": ("F06", "F07", "F07", "F09"),
    "a11": ("F07", "F09", "F09", "F10"),
    "m01": ("F09", "F10", "F10", "F11"),
    "m21": ("F10", "F11", "F11", "F13"),
    "m11": ("F11", "F13", "F13", "F15"),
    "m31": ("F13", "F15", "F15", "F16"),
}
RETURN = {
    "m01": ("B12", "B13", "B13", "B15"),
    "m21": ("B13", "B15", "B15", "B16"),
    "m11": ("B15", "B16", "B16", "B18"),
    "m31": ("B16", "B18", "B18", "B1X"),
    "a01": ("B18", "B1X", "B1X", "B01"),
    "a11": ("B1X", "B01", "B02", "B04"),
    "m00": ("B02", "B04", "B04", "B05"),
    "m20": ("B04", "B05", "B05", "B06"),
    "m10": ("B05", "B06", "B06", "B08"),
    "m30": ("B06", "B08", "B08", "B0X"),
    "a00": ("B08", "B0X", "B0X", "E1"),
    "a10": ("B0X", "E1", "E1", "E2"),
}
HOME = {
    "m0": ("B06", "B0X"),
    "m1": ("B0X", "E2"),
}


def body(
    boundary, segment_ids, w_query, key_projection, value_projection, w_out, w_gate, w_up, w_down,
    attn_gain, mlp_gain, query_gain, key_norm_gain,
):
    s, h, t, g, y, k = (lax.axis_index(name) for name in ("s", "h", "t", "g", "y", "k"))
    groups = lax.axis_size("g")
    micro, tok, width = boundary.shape[1:]
    cols = lax.axis_size("y") * lax.axis_size("k")
    model = width * cols
    head = query_gain.shape[1]
    span = segment_ids.shape[1]
    rb = w_query.shape[1]
    ff = w_gate.shape[2] // 4
    scale_qk = head ** (-0.5)
    clock = Clock()

    packed = jnp.concatenate([attn_gain[0], mlp_gain[0], query_gain[0], key_norm_gain[0]])[None]
    packed = pair(s, packed, swap(packed, "s"))

    rows = boundary[0].reshape(2, 2 * tok, width)
    rows = pair(y, take(rows, y), swap(take(rows, 1 - y), "y")).reshape(2, 2, 2, tok // 2, width)
    rows = pair(k, take(rows, k, 2), swap(take(rows, 1 - k, 2), "k"))
    rows = jnp.stack(
        [jnp.concatenate([rows[j, i, m] for i in (0, 1) for j in (0, 1)], 1) for m in (0, 1)]
    )

    def quarters(weight):
        size = weight.shape[1] // 4
        return [weight[:, i * size : (i + 1) * size] for i in range(4)]

    def to_groups(value):
        return exchange(value, ("s", "t"))

    a_home = []
    for i, (q, o) in enumerate(zip(quarters(w_query[0]), quarters(w_out[0].T))):
        low = (i // 2) * head
        kv = [w[0, :, low : low + head] for w in (key_projection, value_projection)]
        a_home.append(jnp.concatenate([q, o] + kv, 1))
    a_home, packed = lax.optimization_barrier((plain(jnp.stack(a_home)), packed))
    fetched_a = to_groups(a_home)
    def rolled(value):
        half = value.shape[-1] // 2
        return jnp.where(h == 0, value, jnp.concatenate([value[..., half:], value[..., :half]], -1))

    homes = {}

    def fetch(name):
        clock.add(name, *FETCH[name], lambda: homes[name], to_groups)

    def spread(name):
        i, layer = int(name[1]), int(name[2])
        source, block = ("a", i) if name[0] == "a" else (f"m{i % 2}", i // 2)
        plan = SPREAD[name]

        def start():
            return clock.ready[source][2 * layer + block]

        def onward():
            value = [start(), clock.ready[name + "h"]]
            if groups > 1:
                value = [lax.all_gather(half, "g", axis=0, tiled=True) for half in value]
            clock.ready[name] = jnp.concatenate(value)
            return clock.ready[name]

        clock.add(name + "h", plan[0], plan[1], start, lambda value: swap(value, "h"))
        clock.add(name + "y", plan[2], plan[3], onward, lambda value: swap(value, "y"))

    def places_of(kind):
        count = 2 if kind == "m" else 1
        size = rb // count
        for i in range(4 * groups):
            half, block, group = i // (2 * groups), i // groups % 2, i % groups
            for j in range(count):
                yield block * count + j, (half * groups + group) * size, size

    def weight(kind, layer):
        return [
            jnp.concatenate(
                [
                    clock.ready[f"{kind}{part}{layer}{step}"][low : low + size]
                    for part, low, size in places_of(kind)
                ]
            )
            for step in ("", "y")
        ]

    for name in FETCH:
        fetch(name)
    for name in SPREAD:
        spread(name)

    rows, w_gate, w_up, w_down, segment_ids = lax.optimization_barrier(
        (rows, w_gate, w_up, w_down, segment_ids)
    )
    segments = take(segment_ids, 2 * y + h)
    part = tok // 2
    slots = slots_of(s, t, k, g, groups, part)
    first_run = jnp.sum((segments == 0).astype(jnp.int32))
    filled = jnp.sum((segments >= 0).astype(jnp.int32))

    def segments_at(places):
        return jnp.where(places < first_run, 0, jnp.where(places < filled, 1, -1))

    my_segments = segments_at(slots)
    offsets = slots - jnp.where(slots < first_run, 0, jnp.where(slots < filled, first_run, filled))
    inv_freq = THETA ** (-jnp.arange(0, head, 2, dtype=f32) / head)
    angles = offsets.astype(f32)[:, None] * inv_freq[None, :]
    cosine = jnp.concatenate([jnp.cos(angles)] * 2, 1)
    sine = jnp.concatenate([jnp.sin(angles)] * 2, 1)
    valid = (my_segments[:part] >= 0).astype(f32)
    key_slots = lax.all_gather(slots, "g", axis=0, tiled=True) if groups > 1 else slots
    key_segments = segments_at(key_slots)
    allowed = (my_segments[:, None] == key_segments[None, :]) & (
        key_slots[None, :] <= slots[:, None]
    )

    m_home = [
        jnp.concatenate(pieces, 1)
        for pieces in zip(quarters(w_gate[0]), quarters(w_up[0]), quarters(w_down[0].T))
    ]
    homes.update({
        "m0": plain(jnp.stack([value[: rb // 2] for value in m_home])),
        "m1": plain(jnp.stack([value[rb // 2 :] for value in m_home])),
    })

    own_rows = take(rows, h)
    other_rows = swap(take(rows, 1 - h), "h")
    keep = jnp.where(s == h, own_rows, other_rows)
    passed = jnp.where(s == h, other_rows, own_rows)
    passed = swap(passed, "s")
    entering = rolled(jnp.where(s == 0, keep, passed))
    cotangent = rolled(jnp.where(s == 0, passed, keep))
    packed = pair(k, packed, swap(packed, "k"), 1)
    packed = pair(y, packed, swap(packed, "y"), 1).reshape(2, cols, -1).astype(f32)
    gain_a = rolled(packed[:, :, :width].reshape(2, model))
    gain_m = rolled(packed[:, :, width : 2 * width].reshape(2, model))
    gain_q = packed[:, 0, 2 * width : 2 * width + head]
    gain_k = packed[:, 0, 2 * width + head :]
    clock.flying["a"] = fetched_a
    clock.plans["a"] = (None, "p0", None, None)
    entering, cotangent, gain_a, gain_m, homes["m0"], homes["m1"] = clock.point(
        "p0", (entering, cotangent, gain_a, gain_m, homes["m0"], homes["m1"])
    )
    top = cotangent.astype(f32) * valid[:, None]
    kept = {}
    geometry = [cosine, sine, allowed]

    def all_keys(value):
        return lax.all_gather(value, "g", axis=0, tiled=True) if groups > 1 else value

    def sum_keys(value):
        if groups > 1:
            return lax.psum_scatter(value.astype(bf16), "g", scatter_dimension=0, tiled=True).astype(f32)
        return value

    def scores_of(q, keys):
        scores = jnp.einsum("qhd,khd->hqk", q, keys, preferred_element_type=f32) * scale_qk
        return jnp.where(geometry[2][None], scores, -1e30)

    def forward(layer, residual):
        def at(place):
            return lambda chain: clock.point(f"F{layer}{place}", chain)

        scale_a = rms(residual)
        normed = (residual * scale_a * gain_a[layer]).astype(bf16)
        def head_start(pieces):
            if layer == 0:
                pieces, cosine, sine, allowed = at(1)((pieces, *geometry))
                geometry[:] = [cosine, sine, allowed]
            else:
                pieces = at(1)(pieces)
            if layer == 0:
                for label in ("c1", "c2"):
                    pieces = clock.point(label, pieces)
            return pieces

        xa = at(2)(gather_tokens(normed, head_start))
        wa = weight("a", layer)
        q_raw = jnp.stack([dot(xa, w[:, :head]) for w in wa], 1)
        raw = jnp.stack([dot(xa, w[:, 2 * head :]) for w in wa], 1)
        k_raw = raw[:, :, :head]
        v = raw[:, :, head:].astype(bf16)
        q = rotate(q_raw, gain_q[layer], *geometry[:2]).astype(bf16)
        keys = rotate(k_raw, gain_k[layer], *geometry[:2]).astype(bf16)
        keys, values = all_keys(keys), all_keys(v)
        scores = scores_of(q, keys)
        peak = jnp.max(scores, axis=2, keepdims=True)
        exps = jnp.exp(scores - peak)
        denom = jnp.sum(exps, axis=2, keepdims=True)
        mixing = (exps / denom).astype(bf16)
        lse = peak + jnp.log(denom)
        o = jnp.einsum("hqk,khd->qhd", mixing, values, preferred_element_type=f32)
        o = o.astype(bf16)
        near, far = at(3)(split_product((o[:, 0], o[:, 1]), [w[:, head : 2 * head] for w in wa]))
        middle = residual + scatter_sum(near, far, at(4), at(5))
        scale_m = rms(middle)
        normed = (middle * scale_m * gain_m[layer]).astype(bf16)
        xm = gather_tokens(normed, at(6))
        if layer == 1:
            xm, pieces = lax.optimization_barrier((xm, kept["g3"]))
            xm, kept["g3"] = lax.optimization_barrier((xm, gather_core(pieces)))
        xm = at(7)(xm)
        if layer == 0:
            xm, grad = lax.optimization_barrier((xm, top.astype(bf16)))
            kept["g3"] = gather_near(grad)
        wm = weight("m", layer)
        hidden = []
        for w in wm:
            both = dot(xm, w[:, : 2 * ff])
            hidden.append((both[:, :ff], both[:, ff:]))
        act = [(gate * jax.nn.sigmoid(gate) * up).astype(bf16) for gate, up in hidden]
        kept[layer] = (residual, scale_a, xa, q_raw, k_raw, q, keys, values, lse, o, middle, scale_m, xm, hidden, act, wa, wm)

    def project(layer, act):
        return split_product(act, [w[:, 2 * ff :] for w in kept[layer][-1]])

    partial = {}

    def back(name):
        plan = RETURN[name]
        part, layer = int(name[1]), name[2]

        def rows_of(i):
            rows = rb // (2 if name[0] == "m" else 1)
            lows = [j * rows for j, (index, _, _) in enumerate(places_of(name[0])) if index == part]
            return [
                t_dot(jnp.concatenate([left[:, low : low + rows] for low in lows], 1), right)
                for left, right in partial[name[0] + layer][i]
            ]

        def packed_rows(i):
            return plain(jnp.concatenate([value.astype(bf16) for value in rows_of(i)], 1))

        def other():
            if name in ("a00", "a10"):
                clock.ready["own" + name] = clock.loose["own" + name] = packed_rows(0)
            return packed_rows(1)

        def onward():
            received = clock.ready["back_y" + name].astype(f32)
            if "own" + name in clock.ready:
                total = (clock.ready["own" + name].astype(f32) + received).astype(bf16)
            else:
                total, low = [], 0
                for value in rows_of(0):
                    high = low + value.shape[1]
                    total.append((value + received[:, low:high]).astype(bf16))
                    low = high
                total = plain(jnp.concatenate(total, 1))
            count = total.shape[0] // 2
            mine, other = total[:count], total[count:]
            if groups > 1:
                mine, other = (
                    lax.psum_scatter(half, "g", scatter_dimension=0, tiled=True) for half in (mine, other)
                )
            partial["sum" + name] = mine
            return other

        clock.add("back_y" + name, plan[0], plan[1], other, lambda value: swap(value, "y"))
        clock.add("back_h" + name, plan[2], plan[3], onward, lambda value: swap(value, "h"))

    def summed(name):
        return (partial["sum" + name].astype(f32) + clock.ready["back_h" + name].astype(f32)).astype(bf16)

    def both_layers(name):
        names = ("a0", "a1") if name == "a" else (name, f"m{int(name[1]) + 2}")
        return plain(jnp.stack([summed(f"{part}{layer}") for layer in (0, 1) for part in names]))

    for name in RETURN:
        back(name)
    for name, plan in HOME.items():
        clock.add("home" + name, *plan, lambda name=name: both_layers(name), to_groups)

    def backward(layer, grad_top, g3):
        def at(place):
            return lambda chain: clock.point(f"B{layer}{place}", chain)

        (
            residual, scale_a, xa, q_raw, k_raw, q, keys, values, lse, o, middle, scale_m, xm, hidden,
            act, wa, wm,
        ) = kept[layer]
        d_act = [dot(g3, w[:, 2 * ff :]) for w in wm]
        d_hidden = []
        for grad, (gate, up) in zip(d_act, hidden):
            sig = jax.nn.sigmoid(gate)
            d_gate = (grad * up * sig * (1 + gate * (1 - sig))).astype(bf16)
            d_up = (grad * gate * sig).astype(bf16)
            d_hidden.append(jnp.concatenate([d_gate, d_up], 1))
        partial[f"m{layer}"] = [((xm, d), (g3, a)) for d, a in zip(d_hidden, act)]
        beside = at(4)
        if layer == 0:
            d_hidden, output = at(2)((d_hidden, kept["output"]))
            output = scatter_near(*output)

            def beside(chain):
                chain, kept["output"] = lax.optimization_barrier((chain, output))
                return at(4)(chain)
        else:
            d_hidden = at(2)(d_hidden)
        near, far = split_product(d_hidden, [w[:, : 2 * ff] for w in wm])
        near, far = at(3)((near, far))
        d_xm = scatter_sum(near, far, beside, at(5))
        d_mid, d_gain_m = norm_back(middle, scale_m, gain_m[layer], d_xm)
        d_mid = grad_top + d_mid
        g2 = at(7)(gather_tokens(d_mid.astype(bf16), at(6)))
        d_o = jnp.stack([dot(g2, w[:, head : 2 * head]).astype(bf16) for w in wa], 1)
        mixing = jnp.exp(scores_of(q, keys) - lse)
        d_mix = jnp.einsum("qhd,khd->hqk", d_o, values, preferred_element_type=f32)
        inner = jnp.sum(mixing * d_mix, axis=2, keepdims=True)
        d_scores = (mixing * (d_mix - inner)).astype(bf16)
        d_q = jnp.einsum("hqk,khd->qhd", d_scores, keys, preferred_element_type=f32) * scale_qk
        d_k = jnp.einsum("hqk,qhd->khd", d_scores, q, preferred_element_type=f32) * scale_qk
        d_v = jnp.einsum("hqk,qhd->khd", mixing.astype(bf16), d_o, preferred_element_type=f32)
        d_k, d_v = sum_keys(d_k), sum_keys(d_v)
        _, pull_q = jax.vjp(lambda raw, gain: rotate(raw, gain, *geometry[:2]), q_raw, gain_q[layer])
        _, pull_k = jax.vjp(lambda raw, gain: rotate(raw, gain, *geometry[:2]), k_raw, gain_k[layer])
        d_q_raw, d_gain_q = pull_q(d_q)
        d_k_raw, d_gain_k = pull_k(d_k)
        d_q_raw, d_kv_raw = d_q_raw.astype(bf16), jnp.concatenate([d_k_raw, d_v], 2).astype(bf16)
        d_raw = [d_q_raw[:, 0], d_q_raw[:, 1], d_kv_raw[:, 0], d_kv_raw[:, 1]]
        partial[f"a{layer}"] = [
            ((xa, d_q_raw[:, i]), (g2, o[:, i]), (xa, d_kv_raw[:, i])) for i in (0, 1)
        ]
        near, far = at(8)(split_product(d_raw, [w[:, :head] for w in wa] + [w[:, 2 * head :] for w in wa]))
        d_xa = scatter_sum(near, far, at(9), lambda value: clock.point(f"B{layer}X", value))
        d_res, d_gain_a = norm_back(residual, scale_a, gain_a[layer], d_xa)
        return d_mid + d_res, (d_gain_a, d_gain_m, d_gain_q, d_gain_k)

    forward(0, entering.astype(f32))
    act, kept["g3"] = clock.point("F09", (kept[0][14], kept["g3"]))
    near, far = project(0, act)
    middle = kept[0][10] + scatter_sum(near, far, lambda value: value, lambda value: clock.point("F10", value))
    forward(1, middle.astype(bf16).astype(f32))
    grad, gains1 = backward(1, top, kept["g3"])
    grad = grad.astype(bf16)
    pieces = clock.point("B01", gather_near(grad))
    pieces, act = lax.optimization_barrier((pieces, kept[1][14]))
    kept["output"] = scatter_core(*project(1, act))
    g3 = gather_core(pieces)
    grad, gains0 = backward(0, grad.astype(f32), g3)

    low, high = rolled(grad.astype(bf16)), rolled((kept[1][10] + added(*kept["output"])).astype(bf16))
    keep = jnp.where(s == 0, low, high)
    passed = swap(jnp.where(s == 0, high, low), "s")
    (keep, passed), gains0, gains1 = clock.point("E1", ((keep, passed), gains0, gains1))
    sums = []
    for gains in (gains0, gains1):
        sums += [rolled(gains[0]), rolled(gains[1]), gains[2], gains[3]]
    sums = jnp.concatenate(sums)
    sums = sums.reshape(-1, head)
    sums = sums + swap(sums, "k")
    sums = sums + swap(sums, "s")
    sums = sums + swap(sums, "t")
    keep, passed, sums = clock.point("E2", (keep, passed, sums))
    last = both_layers("a")
    ready = {name: clock.ready["home" + name] for name in HOME}
    last, keep, passed, sums, ready = lax.optimization_barrier((last, keep, passed, sums, ready))
    full_a = to_groups(last)
    mine = jnp.where(s == h, keep, passed)
    other = swap(jnp.where(s == h, passed, keep), "h")
    sums = sums + swap(sums, "y")
    rows = pair(h, mine, other)
    blocks = [jnp.stack([rows[..., (2 * i + j) * width : (2 * i + j + 1) * width] for i in (0, 1)]) for j in (0, 1)]
    mine, other = (jnp.where(k == j, blocks[0], blocks[1]) for j in (0, 1))
    rows = pair(k, mine, swap(other, "k"), 2).reshape(2, 2, tok, width)
    rows = pair(y, take(rows, y), swap(take(rows, 1 - y), "y"))
    section_out = rows.reshape(micro, tok, width)
    sums = sums + swap(sums, "h")
    if groups > 1:
        sums = lax.psum(sums, "g")
    sums = take(sums.reshape(2, -1), s)

    def columns(value):
        return jnp.concatenate([value[i] for i in range(4)], 1).astype(f32)

    full_m = jnp.concatenate([ready["m0"], ready["m1"]], 1)
    full_gate, full_up = columns(full_m[..., :ff]), columns(full_m[..., ff : 2 * ff])
    full_down = columns(full_m[..., 2 * ff :]).T
    full_q = columns(full_a[..., :head])
    full_out = columns(full_a[..., head : 2 * head]).T
    full_kv = full_a[..., 2 * head :].astype(f32)
    full_kv = [full_kv[0] + full_kv[1], full_kv[2] + full_kv[3]]
    full_k, full_v = (
        jnp.concatenate([half[:, i * head : (i + 1) * head] for half in full_kv], 1) for i in (0, 1)
    )
    return (
        section_out.astype(f32)[None],
        full_q[None],
        full_k[None],
        full_v[None],
        full_out[None],
        full_gate[None],
        full_up[None],
        full_down[None],
        sums[None, :model],
        sums[None, model : 2 * model],
        sums[None, 2 * model : 2 * model + head],
        sums[None, 2 * model + head :],
    )


def solution(mesh):
    sections, row_count, col_count = (mesh.shape[name] for name in ("section", "row", "col"))
    shape = (sections, 2, 2, row_count // 4, 2, col_count // 2)
    mesh = Mesh(np.asarray(mesh.devices).reshape(shape), ("s", "h", "t", "g", "y", "k"))
    row, col = ("h", "t", "g"), ("y", "k")
    in_row, in_col = P("s", row, col), P("s", col, row)
    return jax.shard_map(
        body,
        mesh=mesh,
        in_specs=(
            P("s", None, row, col), P(), in_row, in_row, in_row, in_col, in_row, in_row, in_col,
            P("s", col), P("s", col), P("s", None), P("s", None),
        ),
        out_specs=(
            P("s", None, row, col), in_row, in_row, in_row, in_col, in_row, in_row, in_col,
            P("s", None), P("s", None), P("s", None), P("s", None),
        ),
        check_vma=False,
    )
```

```python
import jax
import jax.numpy as jnp
import numpy as np
from jax import lax
from jax.experimental.layout import Layout, with_layout_constraint
from jax.sharding import Mesh
from jax.sharding import PartitionSpec as P

EPS = 1e-06
THETA = 1000000.0
f32 = jnp.float32
bf16 = jnp.bfloat16


def swap(value, axis):
    return lax.ppermute(value, axis, [(0, 1), (1, 0)])


def exchange(value, axes):
    return lax.all_to_all(value, axes, 0, 0, tiled=True)


def take(value, index, axis=0):
    return lax.dynamic_index_in_dim(value, index, axis, keepdims=False)


def pair(bit, mine, other, axis=0):
    low = jnp.where(bit == 0, mine, other)
    high = jnp.where(bit == 0, other, mine)
    return jnp.stack([low, high], axis)


def plain(value):
    return with_layout_constraint(value, Layout(major_to_minor=tuple(range(value.ndim))))


def dot(left, right):
    return jnp.dot(left, right, preferred_element_type=f32)


def dot_t(left, right):
    return lax.dot_general(left, right, (((1,), (1,)), ((), ())), preferred_element_type=f32)


def t_dot(left, right):
    return lax.dot_general(left, right, (((0,), (0,)), ((), ())), preferred_element_type=f32)


def cross(value):
    return lax.ppermute(value, ("s", "t"), [(i, 3 - i) for i in range(4)])


def gather_near(mine):
    return [mine, swap(mine, "s"), swap(mine, "t"), cross(mine)]


def gather_core(pieces):
    core = jnp.concatenate(pieces)
    return jnp.concatenate([core, swap(core, "k")])


def gather_tokens(mine, middle):
    return gather_core(middle(gather_near(mine)))


def slots_of(s, t, k, g, groups, part):
    pieces = []
    for dk in (0, 1):
        for ds, dt in ((0, 0), (1, 0), (0, 1), (1, 1)):
            block = ((s ^ ds) * 2 + (t ^ dt)) * groups + g
            start = block * (2 * part) + (k ^ dk) * part
            pieces.append(start + jnp.arange(part, dtype=jnp.int32))
    return jnp.concatenate(pieces)


def scatter_core(near, far):
    total = near + swap(far, "k").astype(f32)
    part = total.shape[0] // 4
    return total[:part], total[part:].astype(bf16)


def scatter_near(total, far):
    part = total.shape[0]
    return total, [swap(far[:part], "s"), swap(far[part : 2 * part], "t"), cross(far[2 * part :])]


def added(total, pieces):
    return total + sum(piece.astype(f32) for piece in pieces)


def scatter_sum(near, far, middle, last):
    return added(*last(scatter_near(*middle(scatter_core(near, far)))))


def split_product(lefts, rights):
    half = lefts[0].shape[0] // 2
    far = sum(dot_t(left[half:], right) for left, right in zip(lefts, rights)).astype(bf16)
    near = sum(dot_t(left[:half], right) for left, right in zip(lefts, rights))
    return near, far


class Clock:
    def __init__(self):
        self.plans, self.flying, self.ready, self.loose = {}, {}, {}, {}

    def add(self, name, begin, end, make, send):
        self.plans[name] = (begin, end, make, send)

    def split(self, name, value):
        self.ready[name] = [value[i] for i in range(value.shape[0])]
        self.loose[name] = self.ready[name]

    def point(self, label, chain):
        ends = [name for name, plan in self.plans.items() if plan[1] == label]
        if ends or self.loose:
            flying = [self.flying[name] for name in ends]
            chain, arrived, loose = lax.optimization_barrier((chain, flying, self.loose))
            self.ready.update(loose)
            self.loose = {}
            for name, value in zip(ends, arrived):
                if name in FETCH or name == "a":
                    self.split(name, value)
                else:
                    self.ready[name] = value
        begins = [name for name, plan in self.plans.items() if plan[0] == label]
        if begins:
            values = [self.plans[name][2]() for name in begins]
            passed, values = lax.optimization_barrier((chain, values))
            if label[0] == "E":
                chain = passed
            for name, value in zip(begins, values):
                self.flying[name] = self.plans[name][3](value)
        return chain


def rms(residual):
    return lax.rsqrt(jnp.mean(residual * residual, axis=1, keepdims=True) + EPS)


def norm_back(residual, scale, gain, grad):
    lifted = grad * gain
    inner = jnp.mean(lifted * residual, axis=1, keepdims=True)
    grad_residual = scale * lifted - residual * (scale**3 * inner)
    return grad_residual, jnp.sum(grad * residual * scale, axis=0)


def rotate(raw, gain, cosine, sine):
    scaled = raw * lax.rsqrt(jnp.mean(raw * raw, axis=2, keepdims=True) + EPS) * gain
    half = raw.shape[2] // 2
    turned = jnp.concatenate([-scaled[:, :, half:], scaled[:, :, :half]], axis=2)
    return scaled * cosine[:, None, :] + turned * sine[:, None, :]


FETCH = {
    "m0": ("F01", "c1"),
    "m1": ("c1", "F03"),
}
SPREAD = {
    "a00": ("p0", "F01", "F01", "c1"),
    "a10": ("F01", "c1", "c1", "c2"),
    "m00": ("c1", "c2", "c2", "F03"),
    "m20": ("c2", "F03", "F03", "F05"),
    "m10": ("F03", "F05", "F05", "F06"),
    "m30": ("F05", "F06", "F06", "F07"),
    "a01": ("F06", "F07", "F07", "F09"),
    "a11": ("F07", "F09", "F09", "F10"),
    "m01": ("F09", "F10", "F10", "F11"),
    "m21": ("F10", "F11", "F11", "F13"),
    "m11": ("F11", "F13", "F13", "F15"),
    "m31": ("F13", "F15", "F15", "F16"),
}
RETURN = {
    "m01": ("B12", "B13", "B13", "B15"),
    "m21": ("B13", "B15", "B15", "B16"),
    "m11": ("B15", "B16", "B16", "B18"),
    "m31": ("B16", "B18", "B18", "B1X"),
    "a01": ("B18", "B1X", "B1X", "B01"),
    "a11": ("B1X", "B01", "B02", "B04"),
    "m00": ("B02", "B04", "B04", "B05"),
    "m20": ("B04", "B05", "B05", "B06"),
    "m10": ("B05", "B06", "B06", "B08"),
    "m30": ("B06", "B08", "B08", "B0X"),
    "a00": ("B08", "B0X", "B0X", "E1"),
    "a10": ("B0X", "E1", "E1", "E2"),
}
HOME = {
    "m0": ("B06", "B0X"),
    "m1": ("B0X", "E2"),
}


def body(
    boundary, segment_ids, w_query, key_projection, value_projection, w_out, w_gate, w_up, w_down,
    attn_gain, mlp_gain, query_gain, key_norm_gain,
):
    s, h, t, g, y, k = (lax.axis_index(name) for name in ("s", "h", "t", "g", "y", "k"))
    groups = lax.axis_size("g")
    micro, tok, width = boundary.shape[1:]
    cols = lax.axis_size("y") * lax.axis_size("k")
    model = width * cols
    head = query_gain.shape[1]
    span = segment_ids.shape[1]
    rb = w_query.shape[1]
    ff = w_gate.shape[2] // 4
    scale_qk = head ** (-0.5)
    clock = Clock()

    packed = jnp.concatenate([attn_gain[0], mlp_gain[0], query_gain[0], key_norm_gain[0]])[None]
    packed = pair(s, packed, swap(packed, "s"))

    rows = boundary[0].reshape(2, 2 * tok, width)
    rows = pair(y, take(rows, y), swap(take(rows, 1 - y), "y")).reshape(2, 2, 2, tok // 2, width)
    rows = pair(k, take(rows, k, 2), swap(take(rows, 1 - k, 2), "k"))
    rows = jnp.stack(
        [jnp.concatenate([rows[j, i, m] for i in (0, 1) for j in (0, 1)], 1) for m in (0, 1)]
    )

    def quarters(weight):
        size = weight.shape[1] // 4
        return [weight[:, i * size : (i + 1) * size] for i in range(4)]

    def to_groups(value):
        return exchange(value, ("s", "t"))

    a_home = []
    for i, (q, o) in enumerate(zip(quarters(w_query[0]), quarters(w_out[0].T))):
        low = (i // 2) * head
        kv = [w[0, :, low : low + head] for w in (key_projection, value_projection)]
        a_home.append(jnp.concatenate([q, o] + kv, 1))
    a_home, packed = lax.optimization_barrier((plain(jnp.stack(a_home)), packed))
    fetched_a = to_groups(a_home)
    def rolled(value):
        half = value.shape[-1] // 2
        return jnp.where(h == 0, value, jnp.concatenate([value[..., half:], value[..., :half]], -1))

    homes = {}

    def fetch(name):
        clock.add(name, *FETCH[name], lambda: homes[name], to_groups)

    def spread(name):
        i, layer = int(name[1]), int(name[2])
        source, block = ("a", i) if name[0] == "a" else (f"m{i % 2}", i // 2)
        plan = SPREAD[name]

        def start():
            return clock.ready[source][2 * layer + block]

        def onward():
            value = [start(), clock.ready[name + "h"]]
            if groups > 1:
                value = [lax.all_gather(half, "g", axis=0, tiled=True) for half in value]
            clock.ready[name] = jnp.concatenate(value)
            return clock.ready[name]

        clock.add(name + "h", plan[0], plan[1], start, lambda value: swap(value, "h"))
        clock.add(name + "y", plan[2], plan[3], onward, lambda value: swap(value, "y"))

    def places_of(kind):
        count = 2 if kind == "m" else 1
        size = rb // count
        for i in range(4 * groups):
            half, block, group = i // (2 * groups), i // groups % 2, i % groups
            for j in range(count):
                yield block * count + j, (half * groups + group) * size, size

    def weight(kind, layer):
        return [
            jnp.concatenate(
                [
                    clock.ready[f"{kind}{part}{layer}{step}"][low : low + size]
                    for part, low, size in places_of(kind)
                ]
            )
            for step in ("", "y")
        ]

    for name in FETCH:
        fetch(name)
    for name in SPREAD:
        spread(name)

    rows, w_gate, w_up, w_down, segment_ids = lax.optimization_barrier(
        (rows, w_gate, w_up, w_down, segment_ids)
    )
    segments = take(segment_ids, 2 * y + h)
    part = tok // 2
    slots = slots_of(s, t, k, g, groups, part)
    first_run = jnp.sum((segments == 0).astype(jnp.int32))
    filled = jnp.sum((segments >= 0).astype(jnp.int32))

    def segments_at(places):
        return jnp.where(places < first_run, 0, jnp.where(places < filled, 1, -1))

    my_segments = segments_at(slots)
    offsets = slots - jnp.where(slots < first_run, 0, jnp.where(slots < filled, first_run, filled))
    inv_freq = THETA ** (-jnp.arange(0, head, 2, dtype=f32) / head)
    angles = offsets.astype(f32)[:, None] * inv_freq[None, :]
    cosine = jnp.concatenate([jnp.cos(angles)] * 2, 1)
    sine = jnp.concatenate([jnp.sin(angles)] * 2, 1)
    valid = (my_segments[:part] >= 0).astype(f32)
    key_slots = lax.all_gather(slots, "g", axis=0, tiled=True) if groups > 1 else slots
    key_segments = segments_at(key_slots)
    allowed = (my_segments[:, None] == key_segments[None, :]) & (
        key_slots[None, :] <= slots[:, None]
    )

    m_home = [
        jnp.concatenate(pieces, 1)
        for pieces in zip(quarters(w_gate[0]), quarters(w_up[0]), quarters(w_down[0].T))
    ]
    homes.update({
        "m0": plain(jnp.stack([value[: rb // 2] for value in m_home])),
        "m1": plain(jnp.stack([value[rb // 2 :] for value in m_home])),
    })

    own_rows = take(rows, h)
    other_rows = swap(take(rows, 1 - h), "h")
    keep = jnp.where(s == h, own_rows, other_rows)
    passed = jnp.where(s == h, other_rows, own_rows)
    passed = swap(passed, "s")
    entering = rolled(jnp.where(s == 0, keep, passed))
    cotangent = rolled(jnp.where(s == 0, passed, keep))
    packed = pair(k, packed, swap(packed, "k"), 1)
    packed = pair(y, packed, swap(packed, "y"), 1).reshape(2, cols, -1).astype(f32)
    gain_a = rolled(packed[:, :, :width].reshape(2, model))
    gain_m = rolled(packed[:, :, width : 2 * width].reshape(2, model))
    gain_q = packed[:, 0, 2 * width : 2 * width + head]
    gain_k = packed[:, 0, 2 * width + head :]
    clock.flying["a"] = fetched_a
    clock.plans["a"] = (None, "p0", None, None)
    entering, cotangent, gain_a, gain_m, homes["m0"], homes["m1"] = clock.point(
        "p0", (entering, cotangent, gain_a, gain_m, homes["m0"], homes["m1"])
    )
    top = cotangent.astype(f32) * valid[:, None]
    kept = {}
    geometry = [cosine, sine, allowed]

    def all_keys(value):
        return lax.all_gather(value, "g", axis=0, tiled=True) if groups > 1 else value

    def sum_keys(value):
        if groups > 1:
            return lax.psum_scatter(value.astype(bf16), "g", scatter_dimension=0, tiled=True).astype(f32)
        return value

    def scores_of(q, keys):
        scores = jnp.einsum("qhd,khd->hqk", q, keys, preferred_element_type=f32) * scale_qk
        return jnp.where(geometry[2][None], scores, -1e30)

    def forward(layer, residual):
        def at(place):
            return lambda chain: clock.point(f"F{layer}{place}", chain)

        scale_a = rms(residual)
        normed = (residual * scale_a * gain_a[layer]).astype(bf16)
        def head_start(pieces):
            if layer == 0:
                pieces, cosine, sine, allowed = at(1)((pieces, *geometry))
                geometry[:] = [cosine, sine, allowed]
            else:
                pieces = at(1)(pieces)
            if layer == 0:
                for label in ("c1", "c2"):
                    pieces = clock.point(label, pieces)
            return pieces

        xa = at(2)(gather_tokens(normed, head_start))
        wa = weight("a", layer)
        q_raw = jnp.stack([dot(xa, w[:, :head]) for w in wa], 1)
        raw = jnp.stack([dot(xa, w[:, 2 * head :]) for w in wa], 1)
        k_raw = raw[:, :, :head]
        v = raw[:, :, head:].astype(bf16)
        q = rotate(q_raw, gain_q[layer], *geometry[:2]).astype(bf16)
        keys = rotate(k_raw, gain_k[layer], *geometry[:2]).astype(bf16)
        keys, values = all_keys(keys), all_keys(v)
        scores = scores_of(q, keys)
        peak = jnp.max(scores, axis=2, keepdims=True)
        exps = jnp.exp(scores - peak)
        denom = jnp.sum(exps, axis=2, keepdims=True)
        mixing = (exps / denom).astype(bf16)
        lse = peak + jnp.log(denom)
        o = jnp.einsum("hqk,khd->qhd", mixing, values, preferred_element_type=f32)
        o = o.astype(bf16)
        near, far = at(3)(split_product((o[:, 0], o[:, 1]), [w[:, head : 2 * head] for w in wa]))
        middle = residual + scatter_sum(near, far, at(4), at(5))
        scale_m = rms(middle)
        normed = (middle * scale_m * gain_m[layer]).astype(bf16)
        xm = gather_tokens(normed, at(6))
        if layer == 1:
            xm, pieces = lax.optimization_barrier((xm, kept["g3"]))
            xm, kept["g3"] = lax.optimization_barrier((xm, gather_core(pieces)))
        xm = at(7)(xm)
        if layer == 0:
            xm, grad = lax.optimization_barrier((xm, top.astype(bf16)))
            kept["g3"] = gather_near(grad)
        wm = weight("m", layer)
        hidden = []
        for w in wm:
            both = dot(xm, w[:, : 2 * ff])
            hidden.append((both[:, :ff], both[:, ff:]))
        act = [(gate * jax.nn.sigmoid(gate) * up).astype(bf16) for gate, up in hidden]
        kept[layer] = (residual, scale_a, xa, q_raw, k_raw, q, keys, values, lse, o, middle, scale_m, xm, hidden, act, wa, wm)

    def project(layer, act):
        return split_product(act, [w[:, 2 * ff :] for w in kept[layer][-1]])

    partial = {}

    def back(name):
        plan = RETURN[name]
        part, layer = int(name[1]), name[2]

        def rows_of(i):
            rows = rb // (2 if name[0] == "m" else 1)
            lows = [j * rows for j, (index, _, _) in enumerate(places_of(name[0])) if index == part]
            return [
                t_dot(jnp.concatenate([left[:, low : low + rows] for low in lows], 1), right)
                for left, right in partial[name[0] + layer][i]
            ]

        def packed_rows(i):
            return plain(jnp.concatenate([value.astype(bf16) for value in rows_of(i)], 1))

        def other():
            if name in ("a00", "a10"):
                clock.ready["own" + name] = clock.loose["own" + name] = packed_rows(0)
            return packed_rows(1)

        def onward():
            received = clock.ready["back_y" + name].astype(f32)
            if "own" + name in clock.ready:
                total = (clock.ready["own" + name].astype(f32) + received).astype(bf16)
            else:
                total, low = [], 0
                for value in rows_of(0):
                    high = low + value.shape[1]
                    total.append((value + received[:, low:high]).astype(bf16))
                    low = high
                total = plain(jnp.concatenate(total, 1))
            count = total.shape[0] // 2
            mine, other = total[:count], total[count:]
            if groups > 1:
                mine, other = (
                    lax.psum_scatter(half, "g", scatter_dimension=0, tiled=True) for half in (mine, other)
                )
            partial["sum" + name] = mine
            return other

        clock.add("back_y" + name, plan[0], plan[1], other, lambda value: swap(value, "y"))
        clock.add("back_h" + name, plan[2], plan[3], onward, lambda value: swap(value, "h"))

    def summed(name):
        return (partial["sum" + name].astype(f32) + clock.ready["back_h" + name].astype(f32)).astype(bf16)

    def both_layers(name):
        names = ("a0", "a1") if name == "a" else (name, f"m{int(name[1]) + 2}")
        return plain(jnp.stack([summed(f"{part}{layer}") for layer in (0, 1) for part in names]))

    for name in RETURN:
        back(name)
    for name, plan in HOME.items():
        clock.add("home" + name, *plan, lambda name=name: both_layers(name), to_groups)

    def backward(layer, grad_top, g3):
        def at(place):
            return lambda chain: clock.point(f"B{layer}{place}", chain)

        (
            residual, scale_a, xa, q_raw, k_raw, q, keys, values, lse, o, middle, scale_m, xm, hidden,
            act, wa, wm,
        ) = kept[layer]
        d_act = [dot(g3, w[:, 2 * ff :]) for w in wm]
        d_hidden = []
        for grad, (gate, up) in zip(d_act, hidden):
            sig = jax.nn.sigmoid(gate)
            d_gate = (grad * up * sig * (1 + gate * (1 - sig))).astype(bf16)
            d_up = (grad * gate * sig).astype(bf16)
            d_hidden.append(jnp.concatenate([d_gate, d_up], 1))
        partial[f"m{layer}"] = [((xm, d), (g3, a)) for d, a in zip(d_hidden, act)]
        beside = at(4)
        if layer == 0:
            d_hidden, output = at(2)((d_hidden, kept["output"]))
            output = scatter_near(*output)

            def beside(chain):
                chain, kept["output"] = lax.optimization_barrier((chain, output))
                return at(4)(chain)
        else:
            d_hidden = at(2)(d_hidden)
        near, far = split_product(d_hidden, [w[:, : 2 * ff] for w in wm])
        near, far = at(3)((near, far))
        d_xm = scatter_sum(near, far, beside, at(5))
        d_mid, d_gain_m = norm_back(middle, scale_m, gain_m[layer], d_xm)
        d_mid = grad_top + d_mid
        g2 = at(7)(gather_tokens(d_mid.astype(bf16), at(6)))
        d_o = jnp.stack([dot(g2, w[:, head : 2 * head]).astype(bf16) for w in wa], 1)
        mixing = jnp.exp(scores_of(q, keys) - lse)
        d_mix = jnp.einsum("qhd,khd->hqk", d_o, values, preferred_element_type=f32)
        inner = jnp.sum(mixing * d_mix, axis=2, keepdims=True)
        d_scores = (mixing * (d_mix - inner)).astype(bf16)
        d_q = jnp.einsum("hqk,khd->qhd", d_scores, keys, preferred_element_type=f32) * scale_qk
        d_k = jnp.einsum("hqk,qhd->khd", d_scores, q, preferred_element_type=f32) * scale_qk
        d_v = jnp.einsum("hqk,qhd->khd", mixing.astype(bf16), d_o, preferred_element_type=f32)
        d_k, d_v = sum_keys(d_k), sum_keys(d_v)
        _, pull_q = jax.vjp(lambda raw, gain: rotate(raw, gain, *geometry[:2]), q_raw, gain_q[layer])
        _, pull_k = jax.vjp(lambda raw, gain: rotate(raw, gain, *geometry[:2]), k_raw, gain_k[layer])
        d_q_raw, d_gain_q = pull_q(d_q)
        d_k_raw, d_gain_k = pull_k(d_k)
        d_q_raw, d_kv_raw = d_q_raw.astype(bf16), jnp.concatenate([d_k_raw, d_v], 2).astype(bf16)
        d_raw = [d_q_raw[:, 0], d_q_raw[:, 1], d_kv_raw[:, 0], d_kv_raw[:, 1]]
        partial[f"a{layer}"] = [
            ((xa, d_q_raw[:, i]), (g2, o[:, i]), (xa, d_kv_raw[:, i])) for i in (0, 1)
        ]
        near, far = at(8)(split_product(d_raw, [w[:, :head] for w in wa] + [w[:, 2 * head :] for w in wa]))
        d_xa = scatter_sum(near, far, at(9), lambda value: clock.point(f"B{layer}X", value))
        d_res, d_gain_a = norm_back(residual, scale_a, gain_a[layer], d_xa)
        return d_mid + d_res, (d_gain_a, d_gain_m, d_gain_q, d_gain_k)

    forward(0, entering.astype(f32))
    act, kept["g3"] = clock.point("F09", (kept[0][14], kept["g3"]))
    near, far = project(0, act)
    middle = kept[0][10] + scatter_sum(near, far, lambda value: value, lambda value: clock.point("F10", value))
    forward(1, middle.astype(bf16).astype(f32))
    grad, gains1 = backward(1, top, kept["g3"])
    grad = grad.astype(bf16)
    pieces = clock.point("B01", gather_near(grad))
    pieces, act = lax.optimization_barrier((pieces, kept[1][14]))
    kept["output"] = scatter_core(*project(1, act))
    g3 = gather_core(pieces)
    grad, gains0 = backward(0, grad.astype(f32), g3)

    low, high = rolled(grad.astype(bf16)), rolled((kept[1][10] + added(*kept["output"])).astype(bf16))
    keep = jnp.where(s == 0, low, high)
    passed = jnp.where(s == 0, high, low)
    (keep, passed), gains0, gains1 = clock.point("E1", ((keep, passed), gains0, gains1))
    passed = swap(passed, "s")
    sums = []
    for gains in (gains0, gains1):
        sums += [rolled(gains[0]), rolled(gains[1]), gains[2], gains[3]]
    sums = jnp.concatenate(sums)
    sums = sums.reshape(-1, head)
    sums = sums + swap(sums, "k")
    sums = sums + swap(sums, "s")
    sums = sums + swap(sums, "t")
    keep, passed, sums = clock.point("E2", (keep, passed, sums))
    last = both_layers("a")
    ready = {name: clock.ready["home" + name] for name in HOME}
    last, keep, passed, sums, ready = lax.optimization_barrier((last, keep, passed, sums, ready))
    full_a = to_groups(last)
    mine = jnp.where(s == h, keep, passed)
    other = swap(jnp.where(s == h, passed, keep), "h")
    sums = sums + swap(sums, "y")
    rows = pair(h, mine, other)
    blocks = [jnp.stack([rows[..., (2 * i + j) * width : (2 * i + j + 1) * width] for i in (0, 1)]) for j in (0, 1)]
    mine, other = (jnp.where(k == j, blocks[0], blocks[1]) for j in (0, 1))
    rows = pair(k, mine, swap(other, "k"), 2).reshape(2, 2, tok, width)
    rows = pair(y, take(rows, y), swap(take(rows, 1 - y), "y"))
    section_out = rows.reshape(micro, tok, width)
    sums = sums + swap(sums, "h")
    if groups > 1:
        sums = lax.psum(sums, "g")
    sums = take(sums.reshape(2, -1), s)

    def columns(value):
        return jnp.concatenate([value[i] for i in range(4)], 1).astype(f32)

    full_m = jnp.concatenate([ready["m0"], ready["m1"]], 1)
    full_gate, full_up = columns(full_m[..., :ff]), columns(full_m[..., ff : 2 * ff])
    full_down = columns(full_m[..., 2 * ff :]).T
    full_q = columns(full_a[..., :head])
    full_out = columns(full_a[..., head : 2 * head]).T
    full_kv = full_a[..., 2 * head :].astype(f32)
    full_kv = [full_kv[0] + full_kv[1], full_kv[2] + full_kv[3]]
    full_k, full_v = (
        jnp.concatenate([half[:, i * head : (i + 1) * head] for half in full_kv], 1) for i in (0, 1)
    )
    return (
        section_out.astype(f32)[None],
        full_q[None],
        full_k[None],
        full_v[None],
        full_out[None],
        full_gate[None],
        full_up[None],
        full_down[None],
        sums[None, :model],
        sums[None, model : 2 * model],
        sums[None, 2 * model : 2 * model + head],
        sums[None, 2 * model + head :],
    )


def solution(mesh):
    sections, row_count, col_count = (mesh.shape[name] for name in ("section", "row", "col"))
    shape = (sections, 2, 2, row_count // 4, 2, col_count // 2)
    mesh = Mesh(np.asarray(mesh.devices).reshape(shape), ("s", "h", "t", "g", "y", "k"))
    row, col = ("h", "t", "g"), ("y", "k")
    in_row, in_col = P("s", row, col), P("s", col, row)
    return jax.shard_map(
        body,
        mesh=mesh,
        in_specs=(
            P("s", None, row, col), P(), in_row, in_row, in_row, in_col, in_row, in_row, in_col,
            P("s", col), P("s", col), P("s", None), P("s", None),
        ),
        out_specs=(
            P("s", None, row, col), in_row, in_row, in_row, in_col, in_row, in_row, in_col,
            P("s", None), P("s", None), P("s", None), P("s", None),
        ),
        check_vma=False,
    )
```
